256 devices in a mesh: dp: 256 (over z, y, x, core).
Axes of the slice: x: 4, y: 4, z: 8, core: 2. Of those that a mesh axis runs over, the one named last changes fastest.
Arguments:
- patches: bfloat16 [2048, 256, 1152], P('dp'), may hold values from -6 to 6
- captions: bfloat16 [2048, 1152], P('dp'), may hold values from -60 to 60
- probe_query: bfloat16 [576], replicated, may hold values from -45 to 45
- key_weight: bfloat16 [1152, 576], replicated, may hold values from -0.1875 to 0.1875
- value_weight: bfloat16 [1152, 576], replicated, may hold values from -0.1875 to 0.1875
- out_weight: bfloat16 [576, 1152], replicated, may hold values from -0.25 to 0.25
- logit_scale: float32 [1], replicated, may hold values from 4 to 16
- logit_bias: float32 [1], replicated, may hold values from -2 to 0
Outputs:
- caption_grad: float32 [2048, 1152], P('dp')
- probe_grad: float32 [576], replicated
- key_grad: bfloat16 [1152, 576], replicated
- value_grad: bfloat16 [1152, 576], replicated
- out_grad: bfloat16 [576, 1152], replicated
The draws below stay inside these ranges and needn't reach their ends.
All inputs are finite; a program needn't handle non-finite values.
Results may differ from the reference program's by a relative error of at most 0.017.
The reference program's roundings to bfloat16 on the way (of `attention_low`, `pooled`, `embedding_grad` and `value_rows_grad`) count: a program that leaves them out, or rounds other values in their place, can miss the bound.
Values may be sent and summed in bfloat16 or wider, within the bound.
A program may use at most 64 MiB of HBM per device.

```python
import math
import jax
import jax.numpy as jnp
from jax import lax

D = 1152
HEADS = 8
HEAD_DIM = 72
PATCHES = 256
CYCLE = 2
IMG_DEV = 8
IMAGES = 2048
N_DP = 256


def draw_captions(key, part):
    key = jax.random.fold_in(key, 11)
    base_key, scale_key = jax.random.split(key)
    base = jnp.clip(jax.random.normal(base_key, (IMAGES, D), jnp.float32), -6.0, 6.0)
    row_scale = jnp.exp(jax.random.uniform(scale_key, (IMAGES, 1), jnp.float32) * math.log(10.0))
    return (base * row_scale).astype(jnp.bfloat16)


def draw_probe_query(key, part):
    key = jax.random.fold_in(key, 7)
    base_key, scale_key = jax.random.split(key)
    base = jnp.clip(jax.random.normal(base_key, (HEADS, HEAD_DIM), jnp.float32), -6.0, 6.0)
    head_scale = jnp.exp(jax.random.uniform(scale_key, (HEADS, 1), jnp.float32) * math.log(3.0))
    return (base * head_scale).reshape(HEADS * HEAD_DIM).astype(jnp.bfloat16)


def steps_of(key, dims, cuts, smallest, top_value):
    def one(position, blocks):
        draws = jax.random.uniform(jax.random.fold_in(jax.random.fold_in(key, 6), position), (blocks,), jnp.float32, smallest / len(cuts), top_value / len(cuts))
        return jnp.repeat(jnp.exp(draws), dims[position] // blocks).reshape((-1,) + (1,) * (len(dims) - position - 1))

    factor_of = one(*cuts[0])
    for cut in cuts[1:]:
        factor_of = factor_of * one(*cut)
    return factor_of


def bell_draw(stream_key, shape, width, bound, pieces=(), kind=jnp.bfloat16):
    drawn = width * jax.random.normal(stream_key, shape, jnp.float32)
    if pieces:
        drawn = drawn * steps_of(stream_key, shape, pieces, -0.22, 0.18)
    return jnp.clip(drawn, -bound, bound).astype(kind)


def setup_inputs(seed: int = 0) -> dict:
    key_list = jax.random.split(jax.random.key(seed), 9)
    patches = bell_draw(key_list[0], (IMAGES, PATCHES, D), 1.0, 6.0, ((0, 256),))
    captions = draw_captions(jax.random.fold_in(key_list[8], 71), 0)
    probe_query = draw_probe_query(jax.random.fold_in(key_list[8], 71), 0)
    key_weight = bell_draw(key_list[3], (D, HEADS * HEAD_DIM), D ** -0.5, 0.1875)
    value_weight = bell_draw(key_list[4], (D, HEADS * HEAD_DIM), D ** -0.5, 0.1875)
    out_weight = bell_draw(key_list[5], (HEADS * HEAD_DIM, D), (HEADS * HEAD_DIM) ** -0.5, 0.25)
    logit_scale = jnp.clip(jnp.exp(jax.random.uniform(key_list[6], (1,), jnp.float32, math.log(4.0), math.log(16.0))), 4.0, 16.0)
    logit_bias = jnp.clip(jax.random.uniform(key_list[7], (1,), jnp.float32, -2.0, 0.0), -2.0, 0.0)
    return {"patches": patches, "captions": captions, "probe_query": probe_query, "key_weight": key_weight, "value_weight": value_weight, "out_weight": out_weight, "logit_scale": logit_scale, "logit_bias": logit_bias}


norm_epsilon = 1e-06

def rounded(values):
    return lax.optimization_barrier(values.astype(jnp.bfloat16))

def normalize(rows):
    length = jnp.sqrt(lax.optimization_barrier(jnp.sum(rows * rows, axis=-1, keepdims=True)) + norm_epsilon)
    return (rows / length, length)

def pool_forward(patch_block, probe, key_weight, value_weight, out_weight):
    count = patch_block.shape[0]
    flat = patch_block.reshape(count * PATCHES, D)
    key_rows = rounded(jnp.dot(flat, key_weight, preferred_element_type=jnp.float32))
    value_rows = rounded(jnp.dot(flat, value_weight, preferred_element_type=jnp.float32))
    key_heads = key_rows.reshape(count, PATCHES, HEADS, HEAD_DIM).astype(jnp.float32)
    value_heads = value_rows.reshape(count, PATCHES, HEADS, HEAD_DIM).astype(jnp.float32)
    scores = jnp.einsum('iphd,hd->ihp', key_heads, probe) / math.sqrt(HEAD_DIM)
    attention = jax.nn.softmax(scores, axis=-1)
    attention_low = rounded(attention).astype(jnp.float32)
    pooled = jnp.einsum('ihp,iphd->ihd', attention_low, value_heads).astype(jnp.bfloat16)
    pooled = pooled.reshape(count, HEADS * HEAD_DIM)
    embedding = jnp.dot(pooled, out_weight, preferred_element_type=jnp.float32)
    return (flat, key_heads, value_heads, attention, pooled, embedding)

def reference(patches, captions, probe_query, key_weight, value_weight, out_weight, logit_scale, logit_bias):
    probe = probe_query.astype(jnp.float32).reshape(HEADS, HEAD_DIM)
    patch_blocks = patches.reshape(N_DP, IMG_DEV, PATCHES, D)

    def embed_block(patch_block):
        return pool_forward(patch_block, probe, key_weight, value_weight, out_weight)[5]
    embeddings = lax.map(embed_block, patch_blocks).reshape(IMAGES, D)
    image_unit, image_length = normalize(embeddings)
    caption_unit, caption_length = normalize(captions.astype(jnp.float32))
    image_blocks = image_unit.reshape(N_DP, IMG_DEV, D)
    caption_blocks = caption_unit.reshape(N_DP, IMG_DEV, D)
    scale = logit_scale[0]
    bias = logit_bias[0]
    highest = lax.Precision.HIGHEST
    image_total = jnp.zeros((N_DP, IMG_DEV, D), jnp.float32)
    caption_total = jnp.zeros((N_DP, IMG_DEV, D), jnp.float32)
    for offset in range(CYCLE + 1):
        visiting = jnp.roll(caption_blocks, offset, axis=0)
        logits = scale * jnp.einsum('bid,bjd->bij', image_blocks, visiting, precision=highest) + bias
        slope = jax.nn.sigmoid(logits)
        if offset == 0:
            slope = slope - jnp.eye(IMG_DEV, dtype=jnp.float32)
        image_total = image_total + scale * jnp.einsum('bij,bjd->bid', slope, visiting, precision=highest)
        back = scale * jnp.einsum('bij,bid->bjd', slope, image_blocks, precision=highest)
        caption_total = caption_total + jnp.roll(back, -offset, axis=0)
    caption_total = caption_total.reshape(IMAGES, D)
    caption_grad = (caption_total - caption_unit * lax.optimization_barrier(jnp.sum(caption_unit * caption_total, axis=-1, keepdims=True))) / caption_length
    image_total = image_total.reshape(IMAGES, D)
    embedding_grad = ((image_total - image_unit * lax.optimization_barrier(jnp.sum(image_unit * image_total, axis=-1, keepdims=True))) / image_length).astype(jnp.bfloat16)
    grad_blocks = embedding_grad.reshape(N_DP, IMG_DEV, D)

    def backward_block(totals, inputs):
        patch_block, block_grad = inputs
        flat, key_heads, value_heads, attention, pooled, embedding = pool_forward(patch_block, probe, key_weight, value_weight, out_weight)
        out_sum = totals[2] + jnp.dot(pooled.T, block_grad, preferred_element_type=jnp.float32)
        pooled_grad = jnp.dot(block_grad, out_weight.T, preferred_element_type=jnp.float32).reshape(IMG_DEV, HEADS, HEAD_DIM)
        attention_grad = jnp.einsum('ihd,iphd->ihp', pooled_grad, value_heads)
        score_grad = attention * (attention_grad - lax.optimization_barrier(jnp.sum(attention * attention_grad, axis=-1, keepdims=True)))
        value_rows_grad = rounded(jnp.einsum('ihp,ihd->iphd', attention, pooled_grad)).reshape(IMG_DEV * PATCHES, HEADS * HEAD_DIM)
        value_sum = totals[1] + jnp.dot(flat.T, value_rows_grad, preferred_element_type=jnp.float32)
        score_low = rounded(score_grad).astype(jnp.float32)
        patch_sum = totals[0] + jnp.einsum('ipc,ihp->ch', flat.reshape(IMG_DEV, PATCHES, D).astype(jnp.float32), score_low)
        probe_sum = totals[3] + jnp.einsum('ihp,iphd->hd', score_grad, key_heads) / math.sqrt(HEAD_DIM)
        return ((patch_sum, value_sum, out_sum, probe_sum), None)
    start = (jnp.zeros((D, HEADS), jnp.float32), jnp.zeros((D, HEADS * HEAD_DIM), jnp.float32), jnp.zeros((HEADS * HEAD_DIM, D), jnp.float32), jnp.zeros((HEADS, HEAD_DIM), jnp.float32))
    totals, unused = lax.scan(backward_block, start, (patch_blocks, grad_blocks))
    key_grad = (totals[0][:, :, None] * probe[None, :, :] / math.sqrt(HEAD_DIM)).reshape(D, HEADS * HEAD_DIM)
    return (caption_grad, totals[3].reshape(HEADS * HEAD_DIM), key_grad.astype(jnp.bfloat16), totals[1].astype(jnp.bfloat16), totals[2].astype(jnp.bfloat16))
```

```python
import functools
import math

import jax
import jax.numpy as jnp
from jax import lax
from jax.experimental import pallas as pl
from jax.experimental.pallas import tpu as pltpu
from jax.sharding import PartitionSpec as P

D = 1152
HEADS = 8
HEAD_DIM = 72
PATCHES = 256
CYCLE = 2
ROWS = HEADS * HEAD_DIM

MESH = pl.DeviceIdType.MESH
HALF = 162
PART = 41
SLOTS = 21
OWNED = 3
GRID = 24
WIDE = 1280


def reduce_kernel(
    value_ref,
    rows_ref,
    small_ref,
    value_out,
    out_out,
    small_out,
    value_send,
    value_got,
    value_own,
    rows_all,
    rows_got,
    small_got,
    small_pair,
    small_all,
    pools,
    out_own,
    first_send,
    first_got,
    grid,
    second_got,
    total,
    third_got,
    owned,
    owned_all,
    small_owned,
    small_slots,
    final,
    pair_sem,
    rows_sem,
    small_sem,
    first_sem,
    second_sem,
    third_sem,
    back_sem,
    back_small_sem,
    spread_sem,
    spread_small_sem,
    home_sem,
    cross_sem,
):
    f32, bf16 = jnp.float32, jnp.bfloat16
    me = lax.axis_index("dp")
    core, x, y, z = me % 2, (me // 2) % 4, (me // 8) % 4, me // 32
    first = x + (y - x) * core
    second = y + (x - y) * core

    def device_at(at_z, at_first, at_second, at_core):
        at_x = at_first + (at_second - at_first) * core
        at_y = at_second + (at_first - at_second) * core
        return ((at_z * 4 + at_y) * 4 + at_x) * 2 + at_core

    other = device_at(z, first, second, 1 - core)

    def first_peer(step):
        place = (first + step) % 4
        return device_at(z, place, second, core), place

    def second_peer(step):
        place = (second + step) % 4
        return device_at(z, first, place, core), place

    def third_peer(step):
        place = (z + step) % 8
        return device_at(place, first, second, core), place

    peers = [other]
    peers += [first_peer(step)[0] for step in (1, 2, 3)]
    peers += [second_peer(step)[0] for step in (1, 2, 3)]
    peers += [third_peer(step)[0] for step in range(1, 8)]
    barrier = pltpu.get_barrier_semaphore()
    for peer in peers:
        pl.semaphore_signal(barrier, inc=1, device_id=(peer,), device_id_type=MESH)
    pl.semaphore_wait(barrier, len(peers))

    sent = []

    def copy_to(device, source, target, sems, slot):
        return pltpu.make_async_remote_copy(
            src_ref=source,
            dst_ref=target,
            send_sem=sems.at[0, slot],
            recv_sem=sems.at[1, slot],
            device_id=(device,),
            device_id_type=MESH,
        )

    def send(*where):
        copy = copy_to(*where)
        copy.start()
        sent.append(copy)
        return copy

    rows_copy = send(other, rows_ref, rows_got, rows_sem, 0)
    small_copy = send(other, small_ref, small_got, small_sem, 0)

    away = (1 - core) * 288
    home = core * 288

    def value_tile(start, row, column):
        at = pl.multiple_of(start + row * 16, 16)
        return value_ref[pl.ds(at, 16), column * 128 : column * 128 + 128]

    value_send[HALF:] = jnp.zeros((2, 16, 128), bf16)
    pair_copies = []
    for row in range(18):
        for column in range(9):
            value_send[row * 9 + column] = value_tile(away, row, column).astype(bf16)
    for k in range(4):
        part = pl.ds(k * PART, PART)
        pair_copies.append(send(other, value_send.at[part], value_got.at[part], pair_sem, k))
    for row in range(18):
        for column in range(9):
            value_own[row * 9 + column] = value_tile(home, row, column)
    value_own[HALF:] = jnp.zeros((2, 16, 128), f32)

    rows_copy.wait_recv()
    small_copy.wait_recv()
    small_pair[...] = small_ref[...] + small_got[...]
    rows_all[0, 0] = rows_ref[...]
    rows_all[0, 1] = rows_got[...]
    gathers = []
    for step in (1, 2, 3):
        device = first_peer(step)[0]
        gathers.append(send(device, rows_all.at[0], rows_all.at[step], rows_sem, step))
        gathers.append(send(device, small_pair, small_all.at[step - 1], small_sem, step))

    for copy in pair_copies:
        copy.wait_recv()
    first_copies = []
    for step in (2, 1, 3):
        device, place = first_peer(step)
        part = pl.ds(place * PART, PART)
        first_send[step - 1] = (value_own[part] + value_got[part].astype(f32)).astype(bf16)
        first_copies.append(
            send(device, first_send.at[step - 1], first_got.at[step - 1], first_sem, step - 1)
        )

    for copy in gathers:
        copy.wait_recv()
    rows = rows_all[...].astype(f32).reshape(8, 16, D)
    embedding_grads = rows[:, :8].reshape(64, D).astype(bf16)
    pools[...] = rows[:, 8:, :ROWS].reshape(64, ROWS).T
    for block in range(3):
        at = pl.multiple_of(home + block * 96, 32)
        term = jnp.dot(
            pools[pl.ds(at, 96), :].astype(bf16), embedding_grads, preferred_element_type=f32
        )
        for row in range(6):
            for column in range(9):
                out_own[(block * 6 + row) * 9 + column] = term[
                    row * 16 : row * 16 + 16, column * 128 : column * 128 + 128
                ]
    out_own[HALF:] = jnp.zeros((2, 16, 128), f32)
    small = small_pair[...] + small_all[0] + small_all[1] + small_all[2]
    grid[:, SLOTS:] = jnp.zeros((4, OWNED, 16, 128), f32)
    for tile in range(5):
        slot = (tile // OWNED, SLOTS + tile % OWNED)
        grid[slot[0], slot[1], 0:8] = small[:, tile * 256 : tile * 256 + 128]
        grid[slot[0], slot[1], 8:16] = small[:, tile * 256 + 128 : tile * 256 + 256]
    mine = first * PART
    grid[1, 20] = out_own[mine]
    grid[2, 0:SLOTS] = out_own[pl.ds(mine + 1, 21)]
    grid[3, 0:19] = out_own[pl.ds(mine + 22, 19)]
    grid[3, 19:SLOTS] = jnp.zeros((2, 16, 128), f32)

    for copy in first_copies:
        copy.wait_recv()

    def value_sum(start, count):
        part = pl.ds(mine + start, count)
        acc = value_own[part] + value_got[part].astype(f32)
        for slot in range(3):
            acc = acc + first_got[slot, start : start + count].astype(f32)
        return acc

    grid[0, 0:SLOTS] = value_sum(0, 21)
    grid[1, 0:20] = value_sum(21, 20)

    second_copies = []
    for step in (2, 1, 3):
        device, place = second_peer(step)
        second_copies.append(
            send(device, grid.at[place], second_got.at[step - 1], second_sem, step - 1)
        )
    for copy in second_copies:
        copy.wait_recv()
    total[...] = grid[second] + second_got[0] + second_got[1] + second_got[2]

    third_copies = []
    for step in (4, 3, 5, 2, 6, 1, 7):
        device, place = third_peer(step)
        third_copies.append(
            send(device, total.at[pl.ds(place * OWNED, OWNED)], third_got.at[step - 1], third_sem, step - 1)
        )
    for copy in third_copies:
        copy.wait_recv()
    result = total[pl.ds(z * OWNED, OWNED)]
    for slot in range(7):
        result = result + third_got[slot]

    owned[...] = result.astype(bf16)
    small_owned[...] = result
    owned_all[pl.ds(z * OWNED, OWNED)] = result.astype(bf16)
    target = owned_all.at[pl.ds(z * OWNED, OWNED)]

    @pl.when(z == 7)
    def _():
        small_slots[second] = result
        for step in range(1, 8):
            device = third_peer(step)[0]
            copy_to(device, small_owned, small_slots.at[second], back_small_sem, step - 1).start()
        for step in range(1, 8):
            device = third_peer(step)[0]
            copy_to(device, small_owned, small_slots.at[second], back_small_sem, step - 1).wait_send()

    @pl.when(z < 7)
    def _():
        for step in (4, 3, 5, 2, 6, 1, 7):
            device = third_peer(step)[0]
            copy_to(device, owned, target, back_sem, step - 1).start()
        for step in range(1, 8):
            device = third_peer(step)[0]
            copy_to(device, owned, target, back_sem, step - 1).wait_send()

    for step in range(1, 8):
        device = third_peer(step)[0]
        source = (z + 8 - step) % 8

        @pl.when(source == 7)
        def _():
            copy_to(device, small_owned, small_slots.at[second], back_small_sem, step - 1).wait_recv()

        @pl.when(source < 7)
        def _():
            arrived = owned_all.at[pl.ds(source * OWNED, OWNED)]
            copy_to(device, owned, arrived, back_sem, step - 1).wait_recv()

    final[core, first, second] = owned_all[0:SLOTS]
    spread = []
    for step in (2, 1, 3):
        device = second_peer(step)[0]
        spread.append(
            send(device, owned_all.at[0:SLOTS], final.at[core, first, second], spread_sem, step - 1)
        )
    for step in (2, 1, 3):
        device = second_peer(step)[0]
        spread.append(
            send(device, small_slots.at[second], small_slots.at[second], spread_small_sem, step - 1)
        )
    for copy in spread:
        copy.wait_recv()

    homes = []
    mine = final.at[core, first]
    for step in (2, 1, 3):
        device = first_peer(step)[0]
        homes.append(send(device, mine, mine, home_sem, step - 1))
    cross = [send(other, mine, mine, cross_sem, 0)]

    for tile in range(5):
        slot = small_slots[tile // OWNED, tile % OWNED]
        small_out[:, tile * 256 : tile * 256 + 128] = slot[0:8]
        small_out[:, tile * 256 + 128 : tile * 256 + 256] = slot[8:16]

    for copy, step in zip(homes[1:] + homes[:1], (1, 3, 2)):
        copy.wait_recv()
        part = final.at[core, (first + 4 - step) % 4]
        cross.append(send(other, part, part, cross_sem, step))

    def unpack(which):
        for tile in range(HALF):
            place, at = tile // PART, tile % PART
            row = pl.ds(pl.multiple_of(which * 288 + tile // 9 * 16, 16), 16)
            column = tile % 9 * 128
            value_out[row, column : column + 128] = final[which, place, at // SLOTS, at % SLOTS]
            at = at + PART
            out_out[row, column : column + 128] = final[which, place, at // SLOTS, at % SLOTS]

    unpack(core)
    for copy in cross:
        copy.wait_recv()
    unpack(1 - core)
    for copy in sent:
        copy.wait_send()


def reduce_all(value_part, rows, small_part):
    f32, bf16 = jnp.float32, jnp.bfloat16
    vmem = pl.BlockSpec(memory_space=pltpu.VMEM)
    dma = pltpu.SemaphoreType.DMA
    return pl.pallas_call(
        reduce_kernel,
        out_shape=(
            jax.ShapeDtypeStruct((ROWS, D), bf16),
            jax.ShapeDtypeStruct((ROWS, D), bf16),
            jax.ShapeDtypeStruct((8, WIDE), f32),
        ),
        in_specs=[vmem] * 3,
        out_specs=[vmem] * 3,
        scratch_shapes=[
            pltpu.VMEM((4 * PART, 16, 128), bf16),
            pltpu.VMEM((4 * PART, 16, 128), bf16),
            pltpu.VMEM((4 * PART, 16, 128), f32),
            pltpu.VMEM((4, 2, 16, D), bf16),
            pltpu.VMEM((16, D), bf16),
            pltpu.VMEM((8, WIDE), f32),
            pltpu.VMEM((8, WIDE), f32),
            pltpu.VMEM((3, 8, WIDE), f32),
            pltpu.VMEM((ROWS, 64), f32),
            pltpu.VMEM((4 * PART, 16, 128), f32),
            pltpu.VMEM((3, PART, 16, 128), bf16),
            pltpu.VMEM((3, PART, 16, 128), bf16),
            pltpu.VMEM((4, GRID, 16, 128), f32),
            pltpu.VMEM((3, GRID, 16, 128), f32),
            pltpu.VMEM((GRID, 16, 128), f32),
            pltpu.VMEM((7, OWNED, 16, 128), f32),
            pltpu.VMEM((OWNED, 16, 128), bf16),
            pltpu.VMEM((GRID, 16, 128), bf16),
            pltpu.VMEM((OWNED, 16, 128), f32),
            pltpu.VMEM((4, OWNED, 16, 128), f32),
            pltpu.VMEM((2, 4, 4, SLOTS, 16, 128), bf16),
            dma((2, 4)),
            dma((2, 4)),
            dma((2, 4)),
            dma((2, 3)),
            dma((2, 3)),
            dma((2, 7)),
            dma((2, 7)),
            dma((2, 7)),
            dma((2, 3)),
            dma((2, 3)),
            dma((2, 3)),
            dma((2, 4)),
        ],
        compiler_params=pltpu.CompilerParams(
            collective_id=0, has_side_effects=True, vmem_limit_bytes=48 * 1024 * 1024
        ),
        name="reduce_all",
    )(value_part, rows, small_part)


norm_epsilon = 1e-06


def passed_along(block, axis, distance):
    devices = range(lax.axis_size(axis))
    route = [((i - distance) % len(devices), i) for i in devices]
    return lax.ppermute(block, axis, route)


def normalize(rows):
    length = jnp.sqrt(jnp.sum(rows * rows, axis=-1, keepdims=True) + norm_epsilon)
    return (rows / length, length)


def on_device(
    patches, captions, probe_query, key_weight, value_weight, out_weight, logit_scale, logit_bias
):
    count = patches.shape[0]
    highest = lax.Precision.HIGHEST
    flat = patches.reshape(count * PATCHES, D)
    probe_low = probe_query.reshape(HEADS, HEAD_DIM)
    key_heads = (
        jnp.dot(flat, key_weight, preferred_element_type=jnp.float32)
        .astype(jnp.bfloat16)
        .reshape(count, PATCHES, HEADS, HEAD_DIM)
    )
    value_heads = (
        jnp.dot(flat, value_weight, preferred_element_type=jnp.float32)
        .astype(jnp.bfloat16)
        .reshape(count, PATCHES, HEADS, HEAD_DIM)
    )
    scores = jnp.einsum(
        "iphd,hd->ihp", key_heads, probe_low, preferred_element_type=jnp.float32
    ) / math.sqrt(HEAD_DIM)
    attention = jax.nn.softmax(scores, axis=-1)
    attention_low = attention.astype(jnp.bfloat16)
    pooled = jnp.einsum(
        "ihp,iphd->ihd", attention_low, value_heads, preferred_element_type=jnp.float32
    ).astype(jnp.bfloat16)
    pooled = pooled.reshape(count, HEADS * HEAD_DIM)
    embedding = jnp.dot(pooled, out_weight, preferred_element_type=jnp.float32)
    image_unit, image_length = normalize(embedding)
    own_unit, own_length = normalize(captions.astype(jnp.float32))
    scale = logit_scale[0]
    bias = logit_bias[0]
    identity = jnp.eye(count, dtype=jnp.float32)
    slope = (
        jax.nn.sigmoid(scale * jnp.dot(image_unit, own_unit.T, precision=highest) + bias) - identity
    )
    image_total = scale * jnp.dot(slope, own_unit, precision=highest)
    own_term = scale * jnp.dot(slope.T, image_unit, precision=highest)
    visiting = captions
    visit_terms = []
    for offset in range(1, CYCLE + 1):
        visiting = passed_along(visiting, "dp", 1)
        visit_unit = normalize(visiting.astype(jnp.float32))[0]
        slope = jax.nn.sigmoid(scale * jnp.dot(image_unit, visit_unit.T, precision=highest) + bias)
        image_total = image_total + scale * jnp.dot(slope, visit_unit, precision=highest)
        visit_terms.append(scale * jnp.dot(slope.T, image_unit, precision=highest))
    carried = own_term
    for offset in range(1, CYCLE + 1):
        carried = passed_along(carried, "dp", 1) + visit_terms[offset - 1]
    caption_total = passed_along(carried, "dp", -CYCLE)
    caption_grad = (
        caption_total - own_unit * jnp.sum(own_unit * caption_total, axis=-1, keepdims=True)
    ) / own_length
    embedding_grad = (
        (image_total - image_unit * jnp.sum(image_unit * image_total, axis=-1, keepdims=True))
        / image_length
    ).astype(jnp.bfloat16)
    pooled_grad = jnp.einsum(
        "nd,kd->nk", embedding_grad, out_weight, preferred_element_type=jnp.float32
    ).reshape(count, HEADS, HEAD_DIM)
    attention_grad = jnp.einsum(
        "ihd,iphd->ihp", pooled_grad, value_heads, preferred_element_type=jnp.float32
    )
    score_grad = attention * (
        attention_grad - jnp.sum(attention * attention_grad, axis=-1, keepdims=True)
    )
    value_rows_grad = (
        jnp.einsum("ihp,ihd->iphd", attention, pooled_grad)
        .astype(jnp.bfloat16)
        .reshape(count * PATCHES, HEADS * HEAD_DIM)
    )
    value_part = jnp.einsum("nk,nc->kc", value_rows_grad, flat, preferred_element_type=jnp.float32)
    score_low = score_grad.astype(jnp.bfloat16)
    patch_part = jnp.einsum("ihp,ipc->hc", score_low, patches, preferred_element_type=jnp.float32)
    probe_part = jnp.einsum(
        "ihp,iphd->hd", score_grad, key_heads, preferred_element_type=jnp.float32
    ) / math.sqrt(HEAD_DIM)
    small_part = jnp.concatenate(
        [patch_part, jnp.pad(probe_part, ((0, 0), (0, WIDE - D - HEAD_DIM)))], axis=1
    )
    rows = jnp.concatenate([embedding_grad, jnp.pad(pooled, ((0, 0), (0, D - ROWS)))], axis=0)
    value_total, out_total, small_total = reduce_all(value_part, rows, small_part)
    probe = probe_query.astype(jnp.float32).reshape(HEADS, HEAD_DIM)
    patch_sum = small_total[:, :D].T
    key_total = (patch_sum[:, :, None] * probe[None, :, :] / math.sqrt(HEAD_DIM)).reshape(D, ROWS)
    return (
        caption_grad,
        small_total[:, D : D + HEAD_DIM].reshape(ROWS),
        key_total.astype(jnp.bfloat16),
        value_total.T,
        out_total,
    )


def solution(mesh):
    placed = (P("dp", None, None), P("dp", None), P(), P(), P(), P(), P(), P())
    return jax.shard_map(
        on_device,
        mesh=mesh,
        in_specs=placed,
        out_specs=(P("dp", None), P(), P(), P(), P()),
        check_vma=False,
    )
```

```python
import math

import jax
import jax.numpy as jnp
from jax import lax
from jax.experimental import pallas as pl
from jax.experimental.pallas import tpu as pltpu
from jax.sharding import PartitionSpec as P

D = 1152
HEADS = 8
HEAD_DIM = 72
PATCHES = 256
IMG_DEV = 8
ROWS = HEADS * HEAD_DIM
FLAT = IMG_DEV * PATCHES
CHUNK = 512

MESH = pl.DeviceIdType.MESH
HALF = 162
HALF_ROWS = 288
PART = 41
SLOTS = 21
OWNED = 3
GRID = 24
WIDE = 1792
SMALL_TILES = WIDE // 256

norm_epsilon = 1e-06


def normalize(rows):
    length = jnp.sqrt(jnp.sum(rows * rows, axis=-1, keepdims=True) + norm_epsilon)
    return (rows / length, length)


def dot(left, right, left_dim=1, right_dim=0, precision=None):
    dims = (((left_dim,), (right_dim,)), ((), ()))
    return lax.dot_general(left, right, dims, precision=precision, preferred_element_type=jnp.float32)


def split_low(values):
    high = values.astype(jnp.bfloat16).astype(jnp.float32)
    return jnp.concatenate([high, values - high], axis=0).astype(jnp.bfloat16)


def whole_kernel(
    scale_ref,
    bias_ref,
    patches_ref,
    captions_ref,
    probe_ref,
    key_ref,
    value_ref,
    out_ref,
    caption_out,
    key_out,
    probe_out,
    value_out,
    out_out,
    x_all,
    key_weight,
    value_weight,
    out_weight,
    keys,
    values,
    scores,
    attention,
    units,
    backs,
    backs_got,
    turned,
    rows_wide,
    rows_own,
    away_rows,
    home_rows,
    score_rows,
    small_own,
    value_send,
    value_got,
    value_own,
    rows_all,
    rows_got,
    small_got,
    small_pair,
    small_all,
    pools,
    out_own,
    first_send,
    first_got,
    grid,
    second_got,
    total,
    third_got,
    owned,
    owned_all,
    small_owned,
    small_slots,
    final,
    load_sem,
    unit_sem,
    visit_sem,
    pair_sem,
    rows_sem,
    small_sem,
    first_sem,
    second_sem,
    third_sem,
    back_sem,
    back_small_sem,
    spread_sem,
    spread_small_sem,
    home_sem,
    cross_sem,
):
    f32, bf16 = jnp.float32, jnp.bfloat16
    highest = lax.Precision.HIGHEST
    me = lax.axis_index("dp")
    core, x, y, z = me % 2, (me // 2) % 4, (me // 8) % 4, me // 32
    first = x + (y - x) * core
    second = y + (x - y) * core

    def device_at(at_z, at_first, at_second, at_core):
        at_x = at_first + (at_second - at_first) * core
        at_y = at_second + (at_first - at_second) * core
        return ((at_z * 4 + at_y) * 4 + at_x) * 2 + at_core

    other = device_at(z, first, second, 1 - core)

    def first_peer(step):
        place = (first + step) % 4
        return device_at(z, place, second, core), place

    def second_peer(step):
        place = (second + step) % 4
        return device_at(z, first, place, core), place

    def third_peer(step):
        place = (z + step) % 8
        return device_at(place, first, second, core), place

    peers = [other]
    peers += [first_peer(step)[0] for step in (1, 2, 3)]
    peers += [second_peer(step)[0] for step in (1, 2, 3)]
    peers += [third_peer(step)[0] for step in range(1, 8)]
    peers += [(me + step) % 256 for step in (1, 2, 254, 255)]
    barrier = pltpu.get_barrier_semaphore()
    for peer in peers:
        pl.semaphore_signal(barrier, inc=1, device_id=(peer,), device_id_type=MESH)

    def load(source, target, slot):
        return pltpu.make_async_copy(source, target, load_sem.at[slot])

    def load_rows(slot):
        part = pl.ds(pl.multiple_of(slot * CHUNK, CHUNK), CHUNK)
        return load(patches_ref.at[part], x_all.at[part], slot)

    load(key_ref, key_weight, 4).start()
    load_rows(0).start()
    load(value_ref, value_weight, 5).start()
    for slot in (1, 2, 3):
        load_rows(slot).start()
    load(out_ref, out_weight, 6).start()

    sent = []

    def copy_to(device, source, target, sems, slot):
        return pltpu.make_async_remote_copy(
            src_ref=source,
            dst_ref=target,
            send_sem=sems.at[0, slot],
            recv_sem=sems.at[1, slot],
            device_id=(device,),
            device_id_type=MESH,
        )

    def send(*where):
        copy = copy_to(*where)
        copy.start()
        sent.append(copy)
        return copy

    head = lax.broadcasted_iota(jnp.int32, (HEADS, ROWS), 0) * HEAD_DIM
    column = lax.broadcasted_iota(jnp.int32, (HEADS, ROWS), 1)
    own_head = (column >= head) & (column < head + HEAD_DIM)
    probe = jnp.where(own_head, jnp.broadcast_to(probe_ref[...].astype(f32), (HEADS, ROWS)), 0.0)
    probe_low = probe.astype(bf16)

    def project(step, unused):
        load_rows(step).wait()
        part = pl.ds(pl.multiple_of(step * CHUNK, CHUNK), CHUNK)
        rows = x_all[part, :]
        key_rows = dot(rows, key_weight[...]).astype(bf16)
        keys[part, :] = key_rows
        values[part, :] = dot(rows, value_weight[...]).astype(bf16)
        score = dot(probe_low, key_rows, 1, 1)
        at = pl.multiple_of(step * 16, 16)
        scores[pl.ds(at, 8), :] = score[:, :PATCHES]
        scores[pl.ds(at + 8, 8), :] = score[:, PATCHES:]
        return unused

    load(key_ref, key_weight, 4).wait()
    load(value_ref, value_weight, 5).wait()
    lax.fori_loop(0, 3, project, 0)
    own_unit, own_length = normalize(captions_ref[...].astype(f32))
    units[0] = own_unit
    pl.semaphore_wait(barrier, len(peers))
    unit_copies = [
        send((me + step) % 256, units.at[0], units.at[step], unit_sem, step - 1) for step in (1, 2)
    ]
    lax.fori_loop(3, 4, project, 0)

    score = scores[...] / math.sqrt(HEAD_DIM)
    raised = jnp.exp(score - jnp.max(score, axis=-1, keepdims=True))
    attend = raised / jnp.sum(raised, axis=-1, keepdims=True)
    attention[...] = attend
    pooled = []
    for image in range(IMG_DEV):
        weights = attend[image * 8 : image * 8 + 8].astype(bf16)
        mixed = dot(weights, values[image * PATCHES : (image + 1) * PATCHES, :])
        pooled.append(jnp.sum(jnp.where(own_head, mixed, 0.0), axis=0, keepdims=True))
    pooled = jnp.concatenate(pooled, axis=0)
    load(out_ref, out_weight, 6).wait()
    embedding = dot(pooled.astype(bf16), out_weight[...])
    image_unit, image_length = normalize(embedding)

    for copy in unit_copies:
        copy.wait_recv()
    caption_units = units[...].reshape(24, D)
    scale, bias = scale_ref[0], bias_ref[0]
    logits = scale * dot(image_unit, caption_units, 1, 1, highest) + bias
    same = lax.broadcasted_iota(jnp.int32, (8, 24), 0) == lax.broadcasted_iota(jnp.int32, (8, 24), 1)
    slope = jax.nn.sigmoid(logits) - jnp.where(same, 1.0, 0.0)
    image_total = scale * dot(slope, caption_units, 1, 0, highest)
    embedding_grad = (
        image_total - image_unit * jnp.sum(image_unit * image_total, axis=-1, keepdims=True)
    ) / image_length
    rows_wide[...] = jnp.zeros((16, D), f32)
    rows_wide[0:8, :] = embedding_grad
    rows_wide[8:16, 0:ROWS] = pooled
    rows_own[...] = rows_wide[...].astype(bf16)
    rows_copy = send(other, rows_own, rows_got, rows_sem, 0)
    backs[...] = (scale * dot(slope, image_unit, 0, 0, highest)).reshape(3, 8, D)
    visit_copies = [
        send((me + 256 - step) % 256, backs.at[step], backs_got.at[step - 1], visit_sem, step - 1)
        for step in (1, 2)
    ]

    grad_low = embedding_grad.astype(bf16)
    pooled_grad = dot(grad_low, out_weight[...], 1, 1)
    turned[...] = dot(out_weight[...], grad_low, 1, 1)
    attention_grad = []
    for image in range(IMG_DEV):
        spread_grad = jnp.where(
            own_head, jnp.broadcast_to(pooled_grad[image : image + 1], (HEADS, ROWS)), 0.0
        )
        both = dot(split_low(spread_grad), values[image * PATCHES : (image + 1) * PATCHES, :], 1, 1)
        attention_grad.append(both[0:8] + both[8:16])
    attention_grad = jnp.concatenate(attention_grad, axis=0)
    score_grad = attend * (
        attention_grad - jnp.sum(attend * attention_grad, axis=-1, keepdims=True)
    )

    def value_rows_grad(start, target):
        for image in range(IMG_DEV):
            for pair in range(2):
                parts = []
                for place in (2 * pair, 2 * pair + 1):
                    at = start + place
                    grads = turned[pl.ds(pl.multiple_of(at * HEAD_DIM, 8), HEAD_DIM), image : image + 1]
                    parts.append(grads * attention[pl.ds(image * 8 + at, 1), :])
                target[pair * 144 : pair * 144 + 144, image * PATCHES : (image + 1) * PATCHES] = (
                    jnp.concatenate(parts, axis=0).astype(bf16)
                )

    value_rows_grad((1 - core) * 4, away_rows)
    for image in range(IMG_DEV):
        part = score_grad[image * 8 : image * 8 + 8]
        lanes = slice(image * PATCHES, (image + 1) * PATCHES)
        away_rows[HALF_ROWS : HALF_ROWS + 16, lanes] = jnp.concatenate(
            [part, jnp.zeros((8, PATCHES), f32)], axis=0
        ).astype(bf16)
        score_rows[:, lanes] = split_low(part)

    rows_copy.wait_recv()
    rows_all[0, 0] = rows_own[...]
    rows_all[0, 1] = rows_got[...]
    gathers = [
        send(first_peer(step)[0], rows_all.at[0], rows_all.at[step], rows_sem, step)
        for step in (1, 2, 3)
    ]

    value_send[HALF:] = jnp.zeros((2, 16, 128), bf16)
    pair_copies = []
    for block in range(5):
        lanes = slice(block * 256, min(block * 256 + 256, D))
        term = dot(away_rows[...], x_all[:, lanes])
        for tile in range(block * 36, min(block * 36 + 36, HALF)):
            row, lane = tile % 18 * 16, tile // 18 * 128 - block * 256
            value_send[tile] = term[row : row + 16, lane : lane + 128].astype(bf16)
        small_own[:, lanes] = term[HALF_ROWS : HALF_ROWS + 8]
        if block > 0:
            part = pl.ds((block - 1) * PART, PART)
            pair_copies.append(
                send(other, value_send.at[part], value_got.at[part], pair_sem, block - 1)
            )
    probe_part = dot(score_rows[...], keys[...])
    probe_part = jnp.where(own_head, probe_part[0:8] + probe_part[8:16], 0.0) / math.sqrt(HEAD_DIM)
    small_own[:, D:WIDE] = jnp.zeros((8, WIDE - D), f32)
    small_own[:, D : D + ROWS] = probe_part
    small_copy = send(other, small_own, small_got, small_sem, 0)

    value_rows_grad(core * 4, home_rows)
    for block in range(5):
        lanes = slice(block * 256, min(block * 256 + 256, D))
        term = dot(home_rows[...], x_all[:, lanes])
        for tile in range(block * 36, min(block * 36 + 36, HALF)):
            row, lane = tile % 18 * 16, tile // 18 * 128 - block * 256
            value_own[tile] = term[row : row + 16, lane : lane + 128]
    value_own[HALF:] = jnp.zeros((2, 16, 128), f32)

    small_copy.wait_recv()
    small_pair[...] = small_own[...] + small_got[...]
    gathers += [
        send(first_peer(step)[0], small_pair, small_all.at[step - 1], small_sem, step)
        for step in (1, 2, 3)
    ]

    for copy in pair_copies:
        copy.wait_recv()
    first_copies = []
    for step in (2, 1, 3):
        device, place = first_peer(step)
        part = pl.ds(place * PART, PART)
        first_send[step - 1] = (value_own[part] + value_got[part].astype(f32)).astype(bf16)
        first_copies.append(
            send(device, first_send.at[step - 1], first_got.at[step - 1], first_sem, step - 1)
        )

    for copy in gathers:
        copy.wait_recv()
    rows = rows_all[...].astype(f32).reshape(8, 16, D)
    embedding_grads = rows[:, :8].reshape(64, D).astype(bf16)
    pools[...] = rows[:, 8:, :ROWS].reshape(64, ROWS).T
    for block in range(3):
        at = pl.multiple_of(core * HALF_ROWS + block * 96, 32)
        term = jnp.dot(
            pools[pl.ds(at, 96), :].astype(bf16), embedding_grads, preferred_element_type=f32
        )
        for row in range(6):
            for column in range(9):
                out_own[column * 18 + block * 6 + row] = term[
                    row * 16 : row * 16 + 16, column * 128 : column * 128 + 128
                ]
    out_own[HALF:] = jnp.zeros((2, 16, 128), f32)
    small = small_pair[...] + small_all[0] + small_all[1] + small_all[2]
    grid[:, SLOTS:] = jnp.zeros((4, OWNED, 16, 128), f32)
    for tile in range(SMALL_TILES):
        slot = (tile // OWNED, SLOTS + tile % OWNED)
        grid[slot[0], slot[1], 0:8] = small[:, tile * 256 : tile * 256 + 128]
        grid[slot[0], slot[1], 8:16] = small[:, tile * 256 + 128 : tile * 256 + 256]
    mine = first * PART
    grid[1, 20] = out_own[mine]
    grid[2, 0:SLOTS] = out_own[pl.ds(mine + 1, 21)]
    grid[3, 0:19] = out_own[pl.ds(mine + 22, 19)]
    grid[3, 19:SLOTS] = jnp.zeros((2, 16, 128), f32)

    for copy in first_copies:
        copy.wait_recv()

    def value_sum(start, count):
        part = pl.ds(mine + start, count)
        acc = value_own[part] + value_got[part].astype(f32)
        for slot in range(3):
            acc = acc + first_got[slot, start : start + count].astype(f32)
        return acc

    grid[0, 0:SLOTS] = value_sum(0, 21)
    grid[1, 0:20] = value_sum(21, 20)

    second_copies = []
    for step in (2, 1, 3):
        device, place = second_peer(step)
        second_copies.append(
            send(device, grid.at[place], second_got.at[step - 1], second_sem, step - 1)
        )
    for copy in second_copies:
        copy.wait_recv()
    total[...] = grid[second] + second_got[0] + second_got[1] + second_got[2]

    third_copies = []
    for step in (4, 3, 5, 2, 6, 1, 7):
        device, place = third_peer(step)
        third_copies.append(
            send(device, total.at[pl.ds(place * OWNED, OWNED)], third_got.at[step - 1], third_sem, step - 1)
        )
    for copy in third_copies:
        copy.wait_recv()
    result = total[pl.ds(z * OWNED, OWNED)]
    for slot in range(7):
        result = result + third_got[slot]

    owned[...] = result.astype(bf16)
    small_owned[...] = result
    owned_all[pl.ds(z * OWNED, OWNED)] = result.astype(bf16)
    target = owned_all.at[pl.ds(z * OWNED, OWNED)]

    @pl.when(z == 7)
    def _():
        small_slots[second] = result
        for step in range(1, 8):
            device = third_peer(step)[0]
            copy_to(device, small_owned, small_slots.at[second], back_small_sem, step - 1).start()
        for step in range(1, 8):
            device = third_peer(step)[0]
            copy_to(device, small_owned, small_slots.at[second], back_small_sem, step - 1).wait_send()

    @pl.when(z < 7)
    def _():
        for step in (4, 3, 5, 2, 6, 1, 7):
            device = third_peer(step)[0]
            copy_to(device, owned, target, back_sem, step - 1).start()
        for step in range(1, 8):
            device = third_peer(step)[0]
            copy_to(device, owned, target, back_sem, step - 1).wait_send()

    for step in range(1, 8):
        device = third_peer(step)[0]
        source = (z + 8 - step) % 8

        @pl.when(source == 7)
        def _():
            copy_to(device, small_owned, small_slots.at[second], back_small_sem, step - 1).wait_recv()

        @pl.when(source < 7)
        def _():
            arrived = owned_all.at[pl.ds(source * OWNED, OWNED)]
            copy_to(device, owned, arrived, back_sem, step - 1).wait_recv()

    final[core, first, second] = owned_all[0:SLOTS]
    spread = []
    for step in (2, 1, 3):
        device = second_peer(step)[0]
        spread.append(
            send(device, owned_all.at[0:SLOTS], final.at[core, first, second], spread_sem, step - 1)
        )
    for step in (2, 1, 3):
        device = second_peer(step)[0]
        spread.append(
            send(device, small_slots.at[second], small_slots.at[second], spread_small_sem, step - 1)
        )
    for copy in spread:
        copy.wait_recv()

    homes = []
    mine = final.at[core, first]
    for step in (2, 1, 3):
        device = first_peer(step)[0]
        homes.append(send(device, mine, mine, home_sem, step - 1))
    cross = [send(other, mine, mine, cross_sem, 0)]

    small = []
    for tile in range(SMALL_TILES):
        slot = small_slots[tile // OWNED, tile % OWNED]
        small += [slot[0:8], slot[8:16]]
    patch_sum = jnp.concatenate(small[:9], axis=1)
    high = patch_sum.astype(bf16).astype(f32)
    middle = (patch_sum - high).astype(bf16).astype(f32)
    thirds = jnp.concatenate([high, middle, patch_sum - high - middle], axis=0).astype(bf16)
    probes = jnp.concatenate([probe] * 3, axis=0).astype(bf16)
    for block in range(3):
        part = slice(block * 384, block * 384 + 384)
        term = dot(thirds[:, part], probes, 0, 0) / math.sqrt(HEAD_DIM)
        key_out[part, :] = term.astype(bf16)
    probe_out[...] = jnp.sum(jnp.concatenate(small[9:], axis=1)[:, :ROWS], axis=0, keepdims=True)
    for copy in visit_copies:
        copy.wait_recv()
    caption_total = backs[0] + backs_got[0] + backs_got[1]
    caption_out[...] = (
        caption_total - own_unit * jnp.sum(own_unit * caption_total, axis=-1, keepdims=True)
    ) / own_length

    for copy, step in zip(homes[1:] + homes[:1], (1, 3, 2)):
        copy.wait_recv()
        part = final.at[core, (first + 4 - step) % 4]
        cross.append(send(other, part, part, cross_sem, step))

    def unpack(which):
        for tile in range(HALF):
            place, at = tile // PART, tile % PART
            row = pl.ds(pl.multiple_of(which * HALF_ROWS + tile % 18 * 16, 16), 16)
            column = tile // 18 * 128
            value_out[row, column : column + 128] = final[which, place, at // SLOTS, at % SLOTS]
            at = at + PART
            out_out[row, column : column + 128] = final[which, place, at // SLOTS, at % SLOTS]

    unpack(core)
    for copy in cross:
        copy.wait_recv()
    unpack(1 - core)
    for copy in sent:
        copy.wait_send()


def on_device(
    patches, captions, probe_query, key_weight, value_weight, out_weight, logit_scale, logit_bias
):
    f32, bf16 = jnp.float32, jnp.bfloat16
    vmem = pl.BlockSpec(memory_space=pltpu.VMEM)
    smem = pl.BlockSpec(memory_space=pltpu.SMEM)
    hbm = pl.BlockSpec(memory_space=pl.ANY)
    dma = pltpu.SemaphoreType.DMA
    caption_grad, key_grad, probe_grad, value_turned, out_grad = pl.pallas_call(
        whole_kernel,
        out_shape=(
            jax.ShapeDtypeStruct((IMG_DEV, D), f32),
            jax.ShapeDtypeStruct((D, ROWS), bf16),
            jax.ShapeDtypeStruct((1, ROWS), f32),
            jax.ShapeDtypeStruct((ROWS, D), bf16),
            jax.ShapeDtypeStruct((ROWS, D), bf16),
        ),
        in_specs=[smem, smem, hbm, vmem, vmem, hbm, hbm, hbm],
        out_specs=[vmem] * 5,
        scratch_shapes=[
            pltpu.VMEM((FLAT, D), bf16),
            pltpu.VMEM((D, ROWS), bf16),
            pltpu.VMEM((D, ROWS), bf16),
            pltpu.VMEM((ROWS, D), bf16),
            pltpu.VMEM((FLAT, ROWS), bf16),
            pltpu.VMEM((FLAT, ROWS), bf16),
            pltpu.VMEM((64, PATCHES), f32),
            pltpu.VMEM((64, PATCHES), f32),
            pltpu.VMEM((3, 8, D), f32),
            pltpu.VMEM((3, 8, D), f32),
            pltpu.VMEM((2, 8, D), f32),
            pltpu.VMEM((ROWS, 8), f32),
            pltpu.VMEM((16, D), f32),
            pltpu.VMEM((16, D), bf16),
            pltpu.VMEM((HALF_ROWS + 16, FLAT), bf16),
            pltpu.VMEM((HALF_ROWS, FLAT), bf16),
            pltpu.VMEM((16, FLAT), bf16),
            pltpu.VMEM((8, WIDE), f32),
            pltpu.VMEM((4 * PART, 16, 128), bf16),
            pltpu.VMEM((4 * PART, 16, 128), bf16),
            pltpu.VMEM((4 * PART, 16, 128), f32),
            pltpu.VMEM((4, 2, 16, D), bf16),
            pltpu.VMEM((16, D), bf16),
            pltpu.VMEM((8, WIDE), f32),
            pltpu.VMEM((8, WIDE), f32),
            pltpu.VMEM((3, 8, WIDE), f32),
            pltpu.VMEM((ROWS, 64), f32),
            pltpu.VMEM((4 * PART, 16, 128), f32),
            pltpu.VMEM((3, PART, 16, 128), bf16),
            pltpu.VMEM((3, PART, 16, 128), bf16),
            pltpu.VMEM((4, GRID, 16, 128), f32),
            pltpu.VMEM((3, GRID, 16, 128), f32),
            pltpu.VMEM((GRID, 16, 128), f32),
            pltpu.VMEM((7, OWNED, 16, 128), f32),
            pltpu.VMEM((OWNED, 16, 128), bf16),
            pltpu.VMEM((GRID, 16, 128), bf16),
            pltpu.VMEM((OWNED, 16, 128), f32),
            pltpu.VMEM((4, OWNED, 16, 128), f32),
            pltpu.VMEM((2, 4, 4, SLOTS, 16, 128), bf16),
            dma((7,)),
            dma((2, 2)),
            dma((2, 2)),
            dma((2, 4)),
            dma((2, 4)),
            dma((2, 4)),
            dma((2, 3)),
            dma((2, 3)),
            dma((2, 7)),
            dma((2, 7)),
            dma((2, 7)),
            dma((2, 3)),
            dma((2, 3)),
            dma((2, 3)),
            dma((2, 4)),
        ],
        compiler_params=pltpu.CompilerParams(
            collective_id=0, has_side_effects=True, vmem_limit_bytes=48 * 1024 * 1024
        ),
        name="whole",
    )(
        logit_scale,
        logit_bias,
        patches.reshape(FLAT, D),
        captions,
        probe_query.reshape(1, ROWS),
        key_weight,
        value_weight,
        out_weight,
    )
    return (caption_grad, probe_grad.reshape(ROWS), key_grad, value_turned.T, out_grad)


def solution(mesh):
    placed = (P("dp", None, None), P("dp", None), P(), P(), P(), P(), P(), P())
    return jax.shard_map(
        on_device,
        mesh=mesh,
        in_specs=placed,
        out_specs=(P("dp", None), P(), P(), P(), P()),
        check_vma=False,
    )
```

```python
import math

import jax
import jax.numpy as jnp
from jax import lax
from jax.experimental import pallas as pl
from jax.experimental.pallas import tpu as pltpu
from jax.sharding import PartitionSpec as P

D = 1152
HEADS = 8
HEAD_DIM = 72
PATCHES = 256
IMG_DEV = 8
ROWS = HEADS * HEAD_DIM
FLAT = IMG_DEV * PATCHES
CHUNK = 512
VALUE_AT = 640

MESH = pl.DeviceIdType.MESH
HALF = 162
HALF_ROWS = 288
PART = 41
PIECE = 11
LIST = 168
OWNED = 2
OWNERS = 6
SLOTS = 14
SMALL_AT = 12
WIDE = 1792
SMALL_TILES = WIDE // 256

norm_epsilon = 1e-06


def normalize(rows):
    length = jnp.sqrt(jnp.sum(rows * rows, axis=-1, keepdims=True) + norm_epsilon)
    return (rows / length, length)


def dot(left, right, left_dim=1, right_dim=0, precision=None):
    dims = (((left_dim,), (right_dim,)), ((), ()))
    return lax.dot_general(left, right, dims, precision=precision, preferred_element_type=jnp.float32)


def split_low(values):
    high = values.astype(jnp.bfloat16).astype(jnp.float32)
    return jnp.concatenate([high, values - high], axis=0).astype(jnp.bfloat16)


def head_mask():
    head = lax.broadcasted_iota(jnp.int32, (HEADS, ROWS), 0) * HEAD_DIM
    column = lax.broadcasted_iota(jnp.int32, (HEADS, ROWS), 1)
    return (column >= head) & (column < head + HEAD_DIM)


def probe_rows(probe_ref, own_head):
    row = probe_ref[...].astype(jnp.float32).reshape(1, ROWS)
    return jnp.where(own_head, jnp.broadcast_to(row, (HEADS, ROWS)), 0.0)


def whole_kernel(
    scale_ref,
    bias_ref,
    patches_ref,
    captions_ref,
    probe_ref,
    key_ref,
    value_ref,
    out_ref,
    caption_out,
    probe_out,
    small_slots,
    value_final,
    out_final,
    x_all,
    captions,
    probe_row,
    weights,
    out_weight,
    keys,
    values,
    scores,
    attention,
    units,
    backs,
    backs_got,
    turned,
    rows_wide,
    rows_own,
    away_rows,
    home_rows,
    score_rows,
    small_own,
    value_send,
    value_got,
    value_own,
    rows_all,
    rows_got,
    small_got,
    small_pair,
    small_all,
    pools,
    out_own,
    first_send,
    first_got,
    value_grid,
    value_second,
    value_total,
    value_third,
    value_owned,
    value_all,
    small_owned,
    out_grid,
    out_second,
    out_total,
    out_third,
    out_owned,
    out_all,
    load_sem,
    unit_sem,
    visit_sem,
    pair_sem,
    rows_sem,
    small_sem,
    first_sem,
    value_second_sem,
    value_third_sem,
    value_back_sem,
    small_back_sem,
    value_spread_sem,
    small_spread_sem,
    value_home_sem,
    value_cross_sem,
    out_second_sem,
    out_third_sem,
    out_back_sem,
    out_spread_sem,
    out_home_sem,
    out_cross_sem,
):
    f32, bf16 = jnp.float32, jnp.bfloat16
    highest = lax.Precision.HIGHEST
    me = lax.axis_index("dp")
    core, x, y, z = me % 2, (me // 2) % 4, (me // 8) % 4, me // 32
    first = x + (y - x) * core
    second = y + (x - y) * core

    def device_at(at_z, at_first, at_second, at_core):
        at_x = at_first + (at_second - at_first) * core
        at_y = at_second + (at_first - at_second) * core
        return ((at_z * 4 + at_y) * 4 + at_x) * 2 + at_core

    other = device_at(z, first, second, 1 - core)

    def first_peer(step):
        place = (first + step) % 4
        return device_at(z, place, second, core), place

    def second_peer(step):
        place = (second + step) % 4
        return device_at(z, first, place, core), place

    def third_peer(step):
        place = (z + step) % 8
        return device_at(place, first, second, core), place

    peers = [other]
    peers += [first_peer(step)[0] for step in (1, 2, 3)]
    peers += [second_peer(step)[0] for step in (1, 2, 3)]
    peers += [third_peer(step)[0] for step in range(1, 8)]
    peers += [(me + step) % 256 for step in (1, 2, 254, 255)]
    barrier = pltpu.get_barrier_semaphore()
    for peer in peers:
        pl.semaphore_signal(barrier, inc=1, device_id=(peer,), device_id_type=MESH)

    def load(source, target, slot):
        return pltpu.make_async_copy(source, target, load_sem.at[slot])

    def load_rows(slot):
        part = pl.ds(pl.multiple_of(slot * CHUNK, CHUNK), CHUNK)
        return load(patches_ref.at[part], x_all.at[part], slot)

    load(key_ref, weights.at[0:ROWS], 4).start()
    load(value_ref, weights.at[VALUE_AT : VALUE_AT + ROWS], 5).start()
    for slot in range(4):
        load_rows(slot).start()
    load(probe_ref, probe_row, 8).start()
    load(captions_ref, captions, 7).start()
    load(out_ref, out_weight, 6).start()
    weights[ROWS:VALUE_AT, :] = jnp.zeros((VALUE_AT - ROWS, D), bf16)

    sent = []

    def copy_to(device, source, target, sems, slot):
        return pltpu.make_async_remote_copy(
            src_ref=source,
            dst_ref=target,
            send_sem=sems.at[0, slot],
            recv_sem=sems.at[1, slot],
            device_id=(device,),
            device_id_type=MESH,
        )

    def send(*where):
        copy = copy_to(*where)
        copy.start()
        sent.append(copy)
        return copy

    own_head = head_mask()
    load(probe_ref, probe_row, 8).wait()
    probe = probe_rows(probe_row, own_head)
    probe_out[...] = probe
    probe_low = probe.astype(bf16)

    def project(step, unused):
        load_rows(step).wait()
        part = pl.ds(pl.multiple_of(step * CHUNK, CHUNK), CHUNK)
        both = dot(x_all[part, :], weights[...], 1, 1)
        key_rows = both[:, :ROWS].astype(bf16)
        keys[part, :] = key_rows
        values[part, :] = both[:, VALUE_AT:].astype(bf16)
        score = dot(probe_low, key_rows, 1, 1)
        at = pl.multiple_of(step * 16, 16)
        scores[pl.ds(at, 8), :] = score[:, :PATCHES]
        scores[pl.ds(at + 8, 8), :] = score[:, PATCHES:]
        return unused

    load(key_ref, weights.at[0:ROWS], 4).wait()
    load(value_ref, weights.at[VALUE_AT : VALUE_AT + ROWS], 5).wait()
    lax.fori_loop(0, 3, project, 0)
    load(captions_ref, captions, 7).wait()
    own_unit, own_length = normalize(captions[...].astype(f32))
    units[0] = own_unit
    pl.semaphore_wait(barrier, len(peers))
    unit_copies = [
        send((me + step) % 256, units.at[0], units.at[step], unit_sem, step - 1) for step in (1, 2)
    ]
    lax.fori_loop(3, 4, project, 0)

    score = scores[...] * (1.0 / math.sqrt(HEAD_DIM))
    raised = jnp.exp(score - jnp.max(score, axis=-1, keepdims=True))
    attend = raised / jnp.sum(raised, axis=-1, keepdims=True)
    attention[...] = attend
    pooled = []
    for image in range(IMG_DEV):
        weights = attend[image * 8 : image * 8 + 8].astype(bf16)
        mixed = dot(weights, values[image * PATCHES : (image + 1) * PATCHES, :])
        pooled.append(jnp.sum(jnp.where(own_head, mixed, 0.0), axis=0, keepdims=True))
    pooled = jnp.concatenate(pooled, axis=0)
    load(out_ref, out_weight, 6).wait()
    embedding = dot(pooled.astype(bf16), out_weight[...])
    image_unit, image_length = normalize(embedding)

    for copy in unit_copies:
        copy.wait_recv()
    caption_units = units[...].reshape(24, D)
    scale, bias = scale_ref[0], bias_ref[0]
    logits = scale * dot(image_unit, caption_units, 1, 1, highest) + bias
    same = lax.broadcasted_iota(jnp.int32, (8, 24), 0) == lax.broadcasted_iota(jnp.int32, (8, 24), 1)
    slope = jax.nn.sigmoid(logits) - jnp.where(same, 1.0, 0.0)
    image_total = scale * dot(slope, caption_units, 1, 0, highest)
    embedding_grad = (
        image_total - image_unit * jnp.sum(image_unit * image_total, axis=-1, keepdims=True)
    ) / image_length
    rows_wide[...] = jnp.zeros((16, D), f32)
    rows_wide[0:8, :] = embedding_grad
    rows_wide[8:16, 0:ROWS] = pooled
    rows_own[...] = rows_wide[...].astype(bf16)
    rows_copy = send(other, rows_own, rows_got, rows_sem, 0)
    backs[...] = (scale * dot(slope, image_unit, 0, 0, highest)).reshape(3, 8, D)
    visit_copies = [
        send((me + 256 - step) % 256, backs.at[step], backs_got.at[step - 1], visit_sem, step - 1)
        for step in (1, 2)
    ]

    grad_low = embedding_grad.astype(bf16)
    pooled_grad = dot(grad_low, out_weight[...], 1, 1)
    turned[...] = dot(out_weight[...], grad_low, 1, 1)
    attention_grad = []
    for image in range(IMG_DEV):
        spread_grad = jnp.where(
            own_head, jnp.broadcast_to(pooled_grad[image : image + 1], (HEADS, ROWS)), 0.0
        )
        both = dot(split_low(spread_grad), values[image * PATCHES : (image + 1) * PATCHES, :], 1, 1)
        attention_grad.append(both[0:8] + both[8:16])
    attention_grad = jnp.concatenate(attention_grad, axis=0)
    score_grad = attend * (
        attention_grad - jnp.sum(attend * attention_grad, axis=-1, keepdims=True)
    )

    rows_copy.wait_recv()
    rows_all[0, 0] = rows_own[...]
    rows_all[0, 1] = rows_got[...]
    row_gathers = [
        send(first_peer(step)[0], rows_all.at[0], rows_all.at[step], rows_sem, step)
        for step in (2, 1, 3)
    ]

    def value_rows_grad(start, target):
        for image in range(IMG_DEV):
            for pair in range(2):
                parts = []
                for place in (2 * pair, 2 * pair + 1):
                    at = start + place
                    grads = turned[pl.ds(pl.multiple_of(at * HEAD_DIM, 8), HEAD_DIM), image : image + 1]
                    parts.append(grads * attention[pl.ds(image * 8 + at, 1), :])
                target[pair * 144 : pair * 144 + 144, image * PATCHES : (image + 1) * PATCHES] = (
                    jnp.concatenate(parts, axis=0).astype(bf16)
                )

    value_rows_grad((1 - core) * 4, away_rows)
    for image in range(IMG_DEV):
        part = score_grad[image * 8 : image * 8 + 8]
        lanes = slice(image * PATCHES, (image + 1) * PATCHES)
        away_rows[HALF_ROWS : HALF_ROWS + 16, lanes] = jnp.concatenate(
            [part, jnp.zeros((8, PATCHES), f32)], axis=0
        ).astype(bf16)
        score_rows[:, lanes] = split_low(part)

    value_send[HALF:] = jnp.zeros((LIST - HALF, 16, 128), bf16)
    pair_copies = []
    for block in range(5):
        lanes = slice(block * 256, min(block * 256 + 256, D))
        term = dot(away_rows[...], x_all[:, lanes])
        for tile in range(block * 36, min(block * 36 + 36, HALF)):
            row, lane = tile % 18 * 16, tile // 18 * 128 - block * 256
            value_send[tile] = term[row : row + 16, lane : lane + 128].astype(bf16)
        small_own[:, lanes] = term[HALF_ROWS : HALF_ROWS + 8]
        if block > 0:
            start = (block - 1) * PART
            part = slice(start, start + PART if block < 4 else LIST)
            pair_copies.append(
                send(other, value_send.at[part], value_got.at[part], pair_sem, block - 1)
            )
    probe_part = dot(score_rows[...], keys[...])
    probe_part = jnp.where(own_head, probe_part[0:8] + probe_part[8:16], 0.0) * (1.0 / math.sqrt(HEAD_DIM))
    small_own[:, D:WIDE] = jnp.zeros((8, WIDE - D), f32)
    small_own[:, D : D + ROWS] = probe_part
    small_copy = send(other, small_own, small_got, small_sem, 0)

    for copy in row_gathers:
        copy.wait_recv()
    rows = rows_all[...].astype(f32).reshape(8, 16, D)
    embedding_grads = rows[:, :8].reshape(64, D).astype(bf16)
    pools[...] = rows[:, 8:, :ROWS].reshape(64, ROWS).T
    for block in range(3):
        at = pl.multiple_of(core * HALF_ROWS + block * 96, 32)
        term = dot(pools[pl.ds(at, 96), :].astype(bf16), embedding_grads)
        for row in range(6):
            for lane in range(9):
                out_own[lane * 18 + block * 6 + row] = term[
                    row * 16 : row * 16 + 16, lane * 128 : lane * 128 + 128
                ]
    out_own[HALF:] = jnp.zeros((LIST - HALF, 16, 128), f32)

    def piece_at(place, piece):
        return pl.ds(place * PART + piece * PIECE, PIECE)

    for piece in range(4):
        out_grid[piece] = out_own[piece_at(first, piece)]
    out_copies = []
    for step in (2, 1, 3):
        device, place = second_peer(step)
        out_copies.append(
            send(device, out_grid.at[place], out_second.at[step - 1], out_second_sem, step - 1)
        )

    value_rows_grad(core * 4, home_rows)
    for block in range(5):
        lanes = slice(block * 256, min(block * 256 + 256, D))
        term = dot(home_rows[...], x_all[:, lanes])
        for tile in range(block * 36, min(block * 36 + 36, HALF)):
            row, lane = tile % 18 * 16, tile // 18 * 128 - block * 256
            value_own[tile] = term[row : row + 16, lane : lane + 128]
    value_own[HALF:] = jnp.zeros((LIST - HALF, 16, 128), f32)

    small_copy.wait_recv()
    small_pair[...] = small_own[...] + small_got[...]
    small_gathers = [
        send(first_peer(step)[0], small_pair, small_all.at[step - 1], small_sem, step)
        for step in (2, 1, 3)
    ]
    for copy in pair_copies:
        copy.wait_recv()
    first_copies = []
    for ahead in (2, 1, 3, 0):
        piece = (second + ahead) % 4
        copies = []
        for step in (2, 1, 3):
            device, place = first_peer(step)
            slot = ahead * 3 + step - 1
            part = piece_at(place, piece)
            first_send[slot] = (value_own[part] + value_got[part].astype(f32)).astype(bf16)
            copies.append(send(device, first_send.at[slot], first_got.at[slot], first_sem, slot))
        first_copies.append((ahead, copies))

    def z_order():
        return (4, 3, 5, 2, 6, 1, 7)

    def send_third(total, got, sems):
        return [
            send(
                third_peer(step)[0],
                total.at[pl.ds(third_peer(step)[1] * OWNED, OWNED)],
                got.at[step - 1],
                sems,
                step - 1,
            )
            for step in z_order()
        ]

    for copy in out_copies:
        copy.wait_recv()
    out_total[0:PIECE] = out_grid[second] + out_second[0] + out_second[1] + out_second[2]
    out_total[PIECE:] = jnp.zeros((16 - PIECE, 16, 128), f32)
    out_thirds = send_third(out_total, out_third, out_third_sem)

    for copy in small_gathers:
        copy.wait_recv()
    small = small_pair[...] + small_all[0] + small_all[1] + small_all[2]
    value_grid[:, PIECE:] = jnp.zeros((4, SLOTS - PIECE, 16, 128), f32)
    for tile in range(SMALL_TILES):
        at = (tile // 2, SMALL_AT + tile % 2)
        value_grid[at[0], at[1], 0:8] = small[:, tile * 256 : tile * 256 + 128]
        value_grid[at[0], at[1], 8:16] = small[:, tile * 256 + 128 : tile * 256 + 256]
    value_copies = []
    for ahead, copies in first_copies:
        for copy in copies:
            copy.wait_recv()
        device, piece = second_peer(ahead)
        part = piece_at(first, piece)
        term = value_own[part] + value_got[part].astype(f32)
        for step in (1, 2, 3):
            term = term + first_got[ahead * 3 + step - 1].astype(f32)
        value_grid[piece, 0:PIECE] = term
        if ahead > 0:
            value_copies.append(
                send(device, value_grid.at[piece], value_second.at[ahead - 1], value_second_sem, ahead - 1)
            )

    def send_back(total, got, copies, owned, every, sems):
        for copy in copies:
            copy.wait_recv()
        mine = pl.ds(z * OWNED, OWNED)
        result = total[mine]
        for slot in range(7):
            result = result + got[slot]
        owned[...] = result.astype(bf16)
        every[mine] = result.astype(bf16)

        @pl.when(z < OWNERS)
        def _():
            for step in z_order():
                copy_to(third_peer(step)[0], owned, every.at[mine], sems, step - 1).start()

        return result

    def end_back(owned, every, sems):
        for step in z_order():
            device = third_peer(step)[0]
            source = (z + 8 - step) % 8

            @pl.when(source < OWNERS)
            def _():
                arrived = every.at[pl.ds(source * OWNED, OWNED)]
                copy_to(device, owned, arrived, sems, step - 1).wait_recv()

            @pl.when(z < OWNERS)
            def _():
                copy_to(device, owned, every.at[pl.ds(z * OWNED, OWNED)], sems, step - 1).wait_send()

    def send_home(part, final, sems, ahead):
        piece = final.at[core, first, part]
        return [
            send(first_peer(step)[0], piece, piece, sems, ahead * 3 + step - 1) for step in (2, 1, 3)
        ]

    def send_spread(every, final, spread_sems, home_sems):
        final[core, first, second] = every[0:PIECE]
        piece = final.at[core, first, second]
        spread = [
            send(second_peer(step)[0], every.at[0:PIECE], piece, spread_sems, step - 1)
            for step in (2, 1, 3)
        ]
        return spread, send_home(second, final, home_sems, 0)

    def forward_spread(spread, final, home_sems):
        homes = []
        for copy, step in zip(spread[1:] + spread[:1], (1, 3, 2)):
            copy.wait_recv()
            homes += send_home((second + 4 - step) % 4, final, home_sems, step)
        return homes

    def forward_homes(homes, final, cross_sems):
        mine = final.at[core, first]
        cross = [send(other, mine, mine, cross_sems, 0)]
        for place, step in ((1, 1), (2, 3), (0, 2)):
            for copy in homes[place::3]:
                copy.wait_recv()
            part = final.at[core, (first + 4 - step) % 4]
            cross.append(send(other, part, part, cross_sems, step))
        return cross

    send_back(out_total, out_third, out_thirds, out_owned, out_all, out_back_sem)

    for copy in value_copies:
        copy.wait_recv()
    value_total[0:SLOTS] = value_grid[second] + value_second[0] + value_second[1] + value_second[2]
    value_total[SLOTS:] = jnp.zeros((16 - SLOTS, 16, 128), f32)
    value_thirds = send_third(value_total, value_third, value_third_sem)

    end_back(out_owned, out_all, out_back_sem)
    out_spread, out_homes = send_spread(out_all, out_final, out_spread_sem, out_home_sem)

    small_sum = send_back(
        value_total, value_third, value_thirds, value_owned, value_all, value_back_sem
    )
    small_owned[...] = small_sum
    mine = small_slots.at[second]

    @pl.when(z == OWNERS)
    def _():
        small_slots[second] = small_sum
        for step in z_order():
            copy_to(third_peer(step)[0], small_owned, mine, small_back_sem, step - 1).start()
        for step in z_order():
            copy_to(third_peer(step)[0], small_owned, mine, small_back_sem, step - 1).wait_send()

    out_homes += forward_spread(out_spread, out_final, out_home_sem)

    end_back(value_owned, value_all, value_back_sem)
    value_spread, value_homes = send_spread(value_all, value_final, value_spread_sem, value_home_sem)

    @pl.when(z != OWNERS)
    def _():
        step = (z + 8 - OWNERS) % 8
        copy_to(third_peer(step)[0], small_owned, mine, small_back_sem, step - 1).wait_recv()

    small_spread = [
        send(second_peer(step)[0], mine, mine, small_spread_sem, step - 1) for step in (2, 1, 3)
    ]
    value_homes += forward_spread(value_spread, value_final, value_home_sem)
    cross = forward_homes(out_homes, out_final, out_cross_sem)

    for copy in visit_copies:
        copy.wait_recv()
    caption_total = backs[0] + backs_got[0] + backs_got[1]
    caption_out[...] = (
        caption_total - own_unit * jnp.sum(own_unit * caption_total, axis=-1, keepdims=True)
    ) / own_length

    cross += forward_homes(value_homes, value_final, value_cross_sem)
    for copy in small_spread + cross:
        copy.wait_recv()
    for copy in sent:
        copy.wait_send()


def finish_kernel(
    probe_ref,
    caption_ref,
    small_ref,
    value_ref,
    out_ref,
    caption_out,
    probe_out,
    key_out,
    value_out,
    out_out,
    key_rows,
    value_rows,
    out_rows,
    store_sem,
):
    f32, bf16 = jnp.float32, jnp.bfloat16

    def store(source, target, slot):
        return pltpu.make_async_copy(source, target, store_sem.at[slot])

    stores = [store(caption_ref, caption_out, 0)]
    stores[0].start()

    def unpack(source, target, sink, slot):
        for core in range(2):
            for tile in range(HALF):
                place, at = tile // PART, tile % PART
                row = core * HALF_ROWS + tile % 18 * 16
                lane = tile // 18 * 128
                target[row : row + 16, lane : lane + 128] = source[core, place, at // PIECE, at % PIECE]
        stores.append(store(target, sink, slot))
        stores[-1].start()

    unpack(value_ref, value_rows, value_out, 1)
    unpack(out_ref, out_rows, out_out, 2)
    small = []
    for tile in range(SMALL_TILES):
        both = small_ref[tile // 2, tile % 2]
        small += [both[0:8], both[8:16]]
    probe_out[...] = jnp.sum(jnp.concatenate(small[9:], axis=1)[:, :ROWS], axis=0, keepdims=True)
    patch_sum = jnp.concatenate(small[:9], axis=1) * (1.0 / math.sqrt(HEAD_DIM))
    probe = probe_ref[...].T
    for pair in range(4):
        parts = []
        for head in (2 * pair, 2 * pair + 1):
            column = probe[head * HEAD_DIM : head * HEAD_DIM + HEAD_DIM, head : head + 1]
            parts.append(column * patch_sum[head : head + 1])
        key_rows[pair * 144 : pair * 144 + 144, :] = jnp.concatenate(parts, axis=0).astype(bf16)
    stores.append(store(key_rows, key_out, 3))
    stores[-1].start()
    for copy in stores:
        copy.wait()


def in_hbm(array):
    return pltpu.with_memory_space_constraint(array, pltpu.HBM)


def on_device(
    patches, captions, probe_query, key_weight, value_weight, out_weight, logit_scale, logit_bias
):
    f32, bf16 = jnp.float32, jnp.bfloat16
    vmem = pl.BlockSpec(memory_space=pltpu.VMEM)
    smem = pl.BlockSpec(memory_space=pltpu.SMEM)
    hbm = pl.BlockSpec(memory_space=pltpu.HBM)
    dma = pltpu.SemaphoreType.DMA
    caption_grad, probe, small, value_final, out_final = pl.pallas_call(
        whole_kernel,
        out_shape=(
            jax.ShapeDtypeStruct((IMG_DEV, D), f32),
            jax.ShapeDtypeStruct((HEADS, ROWS), f32),
            jax.ShapeDtypeStruct((4, OWNED, 16, 128), f32),
            jax.ShapeDtypeStruct((2, 4, 4, PIECE, 16, 128), bf16),
            jax.ShapeDtypeStruct((2, 4, 4, PIECE, 16, 128), bf16),
        ),
        in_specs=[smem, smem, hbm, hbm, hbm, hbm, hbm, hbm],
        out_specs=[vmem] * 5,
        scratch_shapes=[
            pltpu.VMEM((FLAT, D), bf16),
            pltpu.VMEM((IMG_DEV, D), bf16),
            pltpu.VMEM((ROWS,), bf16),
            pltpu.VMEM((VALUE_AT + ROWS, D), bf16),
            pltpu.VMEM((ROWS, D), bf16),
            pltpu.VMEM((FLAT, ROWS), bf16),
            pltpu.VMEM((FLAT, ROWS), bf16),
            pltpu.VMEM((64, PATCHES), f32),
            pltpu.VMEM((64, PATCHES), f32),
            pltpu.VMEM((3, 8, D), f32),
            pltpu.VMEM((3, 8, D), f32),
            pltpu.VMEM((2, 8, D), f32),
            pltpu.VMEM((ROWS, 8), f32),
            pltpu.VMEM((16, D), f32),
            pltpu.VMEM((16, D), bf16),
            pltpu.VMEM((HALF_ROWS + 16, FLAT), bf16),
            pltpu.VMEM((HALF_ROWS, FLAT), bf16),
            pltpu.VMEM((16, FLAT), bf16),
            pltpu.VMEM((8, WIDE), f32),
            pltpu.VMEM((LIST, 16, 128), bf16),
            pltpu.VMEM((LIST, 16, 128), bf16),
            pltpu.VMEM((LIST, 16, 128), f32),
            pltpu.VMEM((4, 2, 16, D), bf16),
            pltpu.VMEM((16, D), bf16),
            pltpu.VMEM((8, WIDE), f32),
            pltpu.VMEM((8, WIDE), f32),
            pltpu.VMEM((3, 8, WIDE), f32),
            pltpu.VMEM((ROWS, 64), f32),
            pltpu.VMEM((LIST, 16, 128), f32),
            pltpu.VMEM((12, PIECE, 16, 128), bf16),
            pltpu.VMEM((12, PIECE, 16, 128), bf16),
            pltpu.VMEM((4, SLOTS, 16, 128), f32),
            pltpu.VMEM((3, SLOTS, 16, 128), f32),
            pltpu.VMEM((16, 16, 128), f32),
            pltpu.VMEM((7, OWNED, 16, 128), f32),
            pltpu.VMEM((OWNED, 16, 128), bf16),
            pltpu.VMEM((16, 16, 128), bf16),
            pltpu.VMEM((OWNED, 16, 128), f32),
            pltpu.VMEM((4, PIECE, 16, 128), f32),
            pltpu.VMEM((3, PIECE, 16, 128), f32),
            pltpu.VMEM((16, 16, 128), f32),
            pltpu.VMEM((7, OWNED, 16, 128), f32),
            pltpu.VMEM((OWNED, 16, 128), bf16),
            pltpu.VMEM((16, 16, 128), bf16),
            dma((9,)),
            dma((2, 2)),
            dma((2, 2)),
            dma((2, 4)),
            dma((2, 4)),
            dma((2, 4)),
            dma((2, 12)),
            dma((2, 3)),
            dma((2, 7)),
            dma((2, 7)),
            dma((2, 7)),
            dma((2, 3)),
            dma((2, 3)),
            dma((2, 12)),
            dma((2, 4)),
            dma((2, 3)),
            dma((2, 7)),
            dma((2, 7)),
            dma((2, 3)),
            dma((2, 12)),
            dma((2, 4)),
        ],
        compiler_params=pltpu.CompilerParams(
            collective_id=0, has_side_effects=True, vmem_limit_bytes=40 * 1024 * 1024
        ),
        name="whole",
    )(
        logit_scale,
        logit_bias,
        in_hbm(patches.reshape(FLAT, D)),
        in_hbm(captions),
        in_hbm(probe_query),
        in_hbm(key_weight.T),
        in_hbm(value_weight.T),
        in_hbm(out_weight),
    )
    caption_grad, probe_grad, key_turned, value_turned, out_grad = pl.pallas_call(
        finish_kernel,
        out_shape=(
            jax.ShapeDtypeStruct((IMG_DEV, D), f32),
            jax.ShapeDtypeStruct((1, ROWS), f32),
            jax.ShapeDtypeStruct((ROWS, D), bf16),
            jax.ShapeDtypeStruct((ROWS, D), bf16),
            jax.ShapeDtypeStruct((ROWS, D), bf16),
        ),
        in_specs=[vmem] * 5,
        out_specs=[hbm, vmem, hbm, hbm, hbm],
        scratch_shapes=[
            pltpu.VMEM((ROWS, D), bf16),
            pltpu.VMEM((ROWS, D), bf16),
            pltpu.VMEM((ROWS, D), bf16),
            dma((4,)),
        ],
        compiler_params=pltpu.CompilerParams(vmem_limit_bytes=16 * 1024 * 1024),
        name="finish",
    )(probe, caption_grad, small, value_final, out_final)
    return (caption_grad, probe_grad.reshape(ROWS), key_turned.T, value_turned.T, out_grad)


def solution(mesh):
    placed = (P("dp", None, None), P("dp", None), P(), P(), P(), P(), P(), P())
    return jax.shard_map(
        on_device,
        mesh=mesh,
        in_specs=placed,
        out_specs=(P("dp", None), P(), P(), P(), P()),
        check_vma=False,
    )
```

```python
import math

import jax
import jax.numpy as jnp
from jax import lax
from jax.experimental import pallas as pl
from jax.experimental.pallas import tpu as pltpu
from jax.sharding import PartitionSpec as P

D = 1152
HEADS = 8
HEAD_DIM = 72
PATCHES = 256
IMG_DEV = 8
ROWS = HEADS * HEAD_DIM
FLAT = IMG_DEV * PATCHES
CHUNK = 512
VALUE_AT = 640

MESH = pl.DeviceIdType.MESH
HALF = 162
HALF_ROWS = 288
PART = 41
PIECE = 11
LIST = 168
OWNED = 2
OWNERS = 6
SLOTS = 14
SMALL_AT = 12
WIDE = 1792
SMALL_TILES = WIDE // 256

norm_epsilon = 1e-06


def normalize(rows):
    length = jnp.sqrt(jnp.sum(rows * rows, axis=-1, keepdims=True) + norm_epsilon)
    return (rows / length, length)


def dot(left, right, left_dim=1, right_dim=0, precision=None):
    dims = (((left_dim,), (right_dim,)), ((), ()))
    return lax.dot_general(left, right, dims, precision=precision, preferred_element_type=jnp.float32)


def split_low(values):
    high = values.astype(jnp.bfloat16).astype(jnp.float32)
    return jnp.concatenate([high, values - high], axis=0).astype(jnp.bfloat16)


def head_mask():
    head = lax.broadcasted_iota(jnp.int32, (HEADS, ROWS), 0) * HEAD_DIM
    column = lax.broadcasted_iota(jnp.int32, (HEADS, ROWS), 1)
    return (column >= head) & (column < head + HEAD_DIM)


def probe_rows(probe_ref, own_head):
    row = probe_ref[...].astype(jnp.float32).reshape(1, ROWS)
    return jnp.where(own_head, jnp.broadcast_to(row, (HEADS, ROWS)), 0.0)


def whole_kernel(
    scale_ref,
    bias_ref,
    patches_ref,
    captions_ref,
    probe_ref,
    key_ref,
    value_ref,
    out_ref,
    caption_out,
    probe_out,
    key_out,
    value_out,
    out_out,
    x_all,
    captions,
    probe_row,
    weights,
    out_weight,
    keys,
    values,
    scores,
    attention,
    units,
    backs,
    backs_got,
    turned,
    rows_wide,
    rows_own,
    away_rows,
    home_rows,
    score_rows,
    small_own,
    value_send,
    value_got,
    value_own,
    rows_all,
    rows_got,
    small_got,
    small_pair,
    small_all,
    pools,
    out_own,
    first_send,
    first_got,
    value_grid,
    value_second,
    value_total,
    value_third,
    value_owned,
    value_all,
    small_owned,
    small_slots,
    value_final,
    out_grid,
    out_second,
    out_total,
    out_third,
    out_owned,
    out_all,
    out_final,
    load_sem,
    link_sem,
):
    f32, bf16 = jnp.float32, jnp.bfloat16
    highest = lax.Precision.HIGHEST
    me = lax.axis_index("dp")
    core, x, y, z = me % 2, (me // 2) % 4, (me // 8) % 4, me // 32
    first = x + (y - x) * core
    second = y + (x - y) * core

    def device_at(at_z, at_first, at_second, at_core):
        at_x = at_first + (at_second - at_first) * core
        at_y = at_second + (at_first - at_second) * core
        return ((at_z * 4 + at_y) * 4 + at_x) * 2 + at_core

    other = device_at(z, first, second, 1 - core)

    def first_peer(step):
        place = (first + step) % 4
        return device_at(z, place, second, core), place

    def second_peer(step):
        place = (second + step) % 4
        return device_at(z, first, place, core), place

    def third_peer(step):
        place = (z + step) % 8
        return device_at(place, first, second, core), place

    peers = [other]
    peers += [first_peer(step)[0] for step in (1, 2, 3)]
    peers += [second_peer(step)[0] for step in (1, 2, 3)]
    peers += [third_peer(step)[0] for step in range(1, 8)]
    peers += [(me + step) % 256 for step in (1, 2, 254, 255)]
    barrier = pltpu.get_barrier_semaphore()
    for peer in peers:
        pl.semaphore_signal(barrier, inc=1, device_id=(peer,), device_id_type=MESH)

    def load(source, target, slot):
        return pltpu.make_async_copy(source, target, load_sem.at[slot])

    def load_rows(slot):
        part = pl.ds(pl.multiple_of(slot * CHUNK, CHUNK), CHUNK)
        return load(patches_ref.at[part], x_all.at[part], slot)

    load(probe_ref, probe_row, 8).start()
    load(key_ref, weights.at[0:ROWS], 4).start()
    load(value_ref, weights.at[VALUE_AT : VALUE_AT + ROWS], 5).start()
    load_rows(0).start()
    load(captions_ref, captions, 7).start()
    for slot in (1, 2, 3):
        load_rows(slot).start()
    load(out_ref, out_weight, 6).start()
    weights[ROWS:VALUE_AT, :] = jnp.zeros((VALUE_AT - ROWS, D), bf16)

    used = []
    ends = []

    def new_sem():
        used.append(None)
        return link_sem.at[len(used) - 1]

    def send(device, source, target, leave, arrive):
        pltpu.make_async_remote_copy(
            src_ref=source,
            dst_ref=target,
            send_sem=leave,
            recv_sem=arrive,
            device_id=(device,),
            device_id_type=MESH,
        ).start()

    def wait(bytes_of, sem):
        pltpu.make_async_copy(bytes_of, bytes_of, sem).wait()

    def send_all(copies, bytes_of):
        leave, arrive = new_sem(), new_sem()
        for device, source, target in copies:
            send(device, source, target, leave, arrive)
        ends.append((bytes_of, leave))
        return bytes_of, arrive

    own_head = head_mask()
    load(probe_ref, probe_row, 8).wait()
    probe = probe_rows(probe_row, own_head)
    probe_low = probe.astype(bf16)

    def project(step, unused):
        load_rows(step).wait()
        part = pl.ds(pl.multiple_of(step * CHUNK, CHUNK), CHUNK)
        both = dot(x_all[part, :], weights[...], 1, 1)
        key_rows = both[:, :ROWS].astype(bf16)
        keys[part, :] = key_rows
        values[part, :] = both[:, VALUE_AT:].astype(bf16)
        score = dot(probe_low, key_rows, 1, 1)
        at = pl.multiple_of(step * 16, 16)
        scores[pl.ds(at, 8), :] = score[:, :PATCHES]
        scores[pl.ds(at + 8, 8), :] = score[:, PATCHES:]
        return unused

    load(key_ref, weights.at[0:ROWS], 4).wait()
    load(value_ref, weights.at[VALUE_AT : VALUE_AT + ROWS], 5).wait()
    lax.fori_loop(0, 3, project, 0)
    load(captions_ref, captions, 7).wait()
    own_unit, own_length = normalize(captions[...].astype(f32))
    units[0] = own_unit
    pl.semaphore_wait(barrier, len(peers))
    unit_copies = send_all(
        [((me + step) % 256, units.at[0], units.at[step]) for step in (1, 2)], units.at[1:3]
    )
    lax.fori_loop(3, 4, project, 0)

    score = scores[...] * (1.0 / math.sqrt(HEAD_DIM))
    raised = jnp.exp(score - jnp.max(score, axis=-1, keepdims=True))
    attend = raised / jnp.sum(raised, axis=-1, keepdims=True)
    attention[...] = attend
    pooled = []
    for image in range(IMG_DEV):
        weights = attend[image * 8 : image * 8 + 8].astype(bf16)
        mixed = dot(weights, values[image * PATCHES : (image + 1) * PATCHES, :])
        pooled.append(jnp.sum(jnp.where(own_head, mixed, 0.0), axis=0, keepdims=True))
    pooled = jnp.concatenate(pooled, axis=0)
    load(out_ref, out_weight, 6).wait()
    embedding = dot(pooled.astype(bf16), out_weight[...])
    image_unit, image_length = normalize(embedding)

    wait(*unit_copies)
    caption_units = units[...].reshape(24, D)
    scale, bias = scale_ref[0], bias_ref[0]
    logits = scale * dot(image_unit, caption_units, 1, 1, highest) + bias
    same = lax.broadcasted_iota(jnp.int32, (8, 24), 0) == lax.broadcasted_iota(jnp.int32, (8, 24), 1)
    slope = jax.nn.sigmoid(logits) - jnp.where(same, 1.0, 0.0)
    image_total = scale * dot(slope, caption_units, 1, 0, highest)
    embedding_grad = (
        image_total - image_unit * jnp.sum(image_unit * image_total, axis=-1, keepdims=True)
    ) / image_length
    rows_wide[...] = jnp.zeros((16, D), f32)
    rows_wide[0:8, :] = embedding_grad
    rows_wide[8:16, 0:ROWS] = pooled
    rows_own[...] = rows_wide[...].astype(bf16)
    rows_copy = send_all([(other, rows_own, rows_got)], rows_got)
    backs[...] = (scale * dot(slope, image_unit, 0, 0, highest)).reshape(3, 8, D)
    visit_copies = send_all(
        [
            ((me + 256 - step) % 256, backs.at[step], backs_got.at[step - 1])
            for step in (1, 2)
        ],
        backs_got,
    )

    grad_low = embedding_grad.astype(bf16)
    pooled_grad = dot(grad_low, out_weight[...], 1, 1)
    turned[...] = dot(out_weight[...], grad_low, 1, 1)
    attention_grad = []
    for image in range(IMG_DEV):
        spread_grad = jnp.where(
            own_head, jnp.broadcast_to(pooled_grad[image : image + 1], (HEADS, ROWS)), 0.0
        )
        both = dot(split_low(spread_grad), values[image * PATCHES : (image + 1) * PATCHES, :], 1, 1)
        attention_grad.append(both[0:8] + both[8:16])
    attention_grad = jnp.concatenate(attention_grad, axis=0)
    score_grad = attend * (
        attention_grad - jnp.sum(attend * attention_grad, axis=-1, keepdims=True)
    )

    wait(*rows_copy)
    rows_all[0, 0] = rows_own[...]
    rows_all[0, 1] = rows_got[...]
    row_gathers = send_all(
        [(first_peer(step)[0], rows_all.at[0], rows_all.at[step]) for step in (2, 1, 3)],
        rows_all.at[1:4],
    )

    def value_rows_grad(start, target):
        for image in range(IMG_DEV):
            for pair in range(2):
                parts = []
                for place in (2 * pair, 2 * pair + 1):
                    at = start + place
                    grads = turned[pl.ds(pl.multiple_of(at * HEAD_DIM, 8), HEAD_DIM), image : image + 1]
                    parts.append(grads * attention[pl.ds(image * 8 + at, 1), :])
                target[pair * 144 : pair * 144 + 144, image * PATCHES : (image + 1) * PATCHES] = (
                    jnp.concatenate(parts, axis=0).astype(bf16)
                )

    value_rows_grad((1 - core) * 4, away_rows)
    for image in range(IMG_DEV):
        part = score_grad[image * 8 : image * 8 + 8]
        lanes = slice(image * PATCHES, (image + 1) * PATCHES)
        away_rows[HALF_ROWS : HALF_ROWS + 16, lanes] = jnp.concatenate(
            [part, jnp.zeros((8, PATCHES), f32)], axis=0
        ).astype(bf16)
        score_rows[:, lanes] = split_low(part)

    value_send[HALF:] = jnp.zeros((LIST - HALF, 16, 128), bf16)
    pair_leave, pair_arrive = new_sem(), new_sem()
    ends.append((value_send, pair_leave))
    for block in range(5):
        lanes = slice(block * 256, min(block * 256 + 256, D))
        term = dot(away_rows[...], x_all[:, lanes])
        for tile in range(block * 36, min(block * 36 + 36, HALF)):
            row, lane = tile % 18 * 16, tile // 18 * 128 - block * 256
            value_send[tile] = term[row : row + 16, lane : lane + 128].astype(bf16)
        small_own[:, lanes] = term[HALF_ROWS : HALF_ROWS + 8]
        if block > 0:
            start = (block - 1) * PART
            part = slice(start, start + PART if block < 4 else LIST)
            send(other, value_send.at[part], value_got.at[part], pair_leave, pair_arrive)
    probe_part = dot(score_rows[...], keys[...])
    probe_part = jnp.where(own_head, probe_part[0:8] + probe_part[8:16], 0.0) * (1.0 / math.sqrt(HEAD_DIM))
    small_own[:, D:WIDE] = jnp.zeros((8, WIDE - D), f32)
    small_own[:, D : D + ROWS] = probe_part
    small_copy = send_all([(other, small_own, small_got)], small_got)

    value_rows_grad(core * 4, home_rows)
    for block in range(5):
        lanes = slice(block * 256, min(block * 256 + 256, D))
        term = dot(home_rows[...], x_all[:, lanes])
        for tile in range(block * 36, min(block * 36 + 36, HALF)):
            row, lane = tile % 18 * 16, tile // 18 * 128 - block * 256
            value_own[tile] = term[row : row + 16, lane : lane + 128]
    value_own[HALF:] = jnp.zeros((LIST - HALF, 16, 128), f32)

    wait(*small_copy)
    small_pair[...] = small_own[...] + small_got[...]
    small_gathers = send_all(
        [(first_peer(step)[0], small_pair, small_all.at[step - 1]) for step in (2, 1, 3)], small_all
    )
    def piece_at(place, piece):
        return pl.ds(place * PART + piece * PIECE, PIECE)

    wait(value_got, pair_arrive)
    first_copies = []
    for ahead in (2, 1, 3, 0):
        piece = (second + ahead) % 4
        copies = []
        for step in (2, 1, 3):
            device, place = first_peer(step)
            slot = ahead * 3 + step - 1
            part = piece_at(place, piece)
            first_send[slot] = (value_own[part] + value_got[part].astype(f32)).astype(bf16)
            copies.append((device, first_send.at[slot], first_got.at[slot]))
        first_copies.append((ahead, send_all(copies, first_got.at[ahead * 3 : ahead * 3 + 3])))

    wait(*row_gathers)
    rows = rows_all[...].astype(f32).reshape(8, 16, D)
    embedding_grads = rows[:, :8].reshape(64, D).astype(bf16)
    pools[...] = rows[:, 8:, :ROWS].reshape(64, ROWS).T
    for block in range(3):
        at = pl.multiple_of(core * HALF_ROWS + block * 96, 32)
        term = dot(pools[pl.ds(at, 96), :].astype(bf16), embedding_grads)
        for row in range(6):
            for lane in range(9):
                out_own[lane * 18 + block * 6 + row] = term[
                    row * 16 : row * 16 + 16, lane * 128 : lane * 128 + 128
                ]
    out_own[HALF:] = jnp.zeros((LIST - HALF, 16, 128), f32)

    for piece in range(4):
        out_grid[piece] = out_own[piece_at(first, piece)]
    out_copies = send_all(
        [
            (second_peer(step)[0], out_grid.at[second_peer(step)[1]], out_second.at[step - 1])
            for step in (2, 1, 3)
        ],
        out_second,
    )

    wait(*small_gathers)
    small = small_pair[...] + small_all[0] + small_all[1] + small_all[2]
    value_grid[:, PIECE:] = jnp.zeros((4, SLOTS - PIECE, 16, 128), f32)
    for tile in range(SMALL_TILES):
        at = (tile // 2, SMALL_AT + tile % 2)
        value_grid[at[0], at[1], 0:8] = small[:, tile * 256 : tile * 256 + 128]
        value_grid[at[0], at[1], 8:16] = small[:, tile * 256 + 128 : tile * 256 + 256]
    value_leave, value_arrive = new_sem(), new_sem()
    for ahead, copies in first_copies:
        wait(*copies)
        device, piece = second_peer(ahead)
        part = piece_at(first, piece)
        term = value_own[part] + value_got[part].astype(f32)
        for step in (1, 2, 3):
            term = term + first_got[ahead * 3 + step - 1].astype(f32)
        value_grid[piece, 0:PIECE] = term
        if ahead > 0:
            send(device, value_grid.at[piece], value_second.at[ahead - 1], value_leave, value_arrive)
    ends.append((value_second, value_leave))

    def z_order():
        return (4, 3, 5, 2, 6, 1, 7)

    def send_third(total, got):
        copies = []
        for step in z_order():
            device, place = third_peer(step)
            copies.append((device, total.at[pl.ds(place * OWNED, OWNED)], got.at[step - 1]))
        return send_all(copies, got)

    def send_back(total, got, copies, owned, every):
        wait(*copies)
        mine = pl.ds(z * OWNED, OWNED)
        result = total[mine]
        for slot in range(7):
            result = result + got[slot]
        owned[...] = result.astype(bf16)
        every[mine] = result.astype(bf16)
        leave, arrive = new_sem(), new_sem()

        @pl.when(z < OWNERS)
        def _():
            for step in z_order():
                send(third_peer(step)[0], owned, every.at[mine], leave, arrive)

        return result, leave, arrive

    def end_back(every, leave, arrive):
        @pl.when(z < OWNERS)
        def _():
            wait(every.at[0 : (OWNERS - 1) * OWNED], arrive)
            wait(every.at[0 : 7 * OWNED], leave)

        @pl.when(z >= OWNERS)
        def _():
            wait(every.at[0 : OWNERS * OWNED], arrive)

    def send_home(part, final, leave, arrives):
        piece = final.at[core, first, part]
        for step in (2, 1, 3):
            send(first_peer(step)[0], piece, piece, leave, arrives[step - 1])

    def send_spread(every, final):
        final[core, first, second] = every[0:PIECE]
        piece = final.at[core, first, second]
        leave, arrives = new_sem(), [new_sem() for _ in range(3)]
        for step in (2, 1, 3):
            send(second_peer(step)[0], every.at[0:PIECE], piece, leave, arrives[step - 1])
        ends.append((final.at[core, first, 0:3], leave))
        home_leave, home_arrives = new_sem(), [new_sem() for _ in range(3)]
        send_home(second, final, home_leave, home_arrives)
        ends.append((final.at[core, 0:3], home_leave))
        return arrives, home_leave, home_arrives

    def forward_spread(final, arrives, home_leave, home_arrives):
        for step in (1, 3, 2):
            place = (second + 4 - step) % 4
            wait(final.at[core, first, place], arrives[step - 1])
            send_home(place, final, home_leave, home_arrives)

    def forward_homes(final, home_arrives):
        leave, arrive = new_sem(), new_sem()
        send(other, final.at[core, first], final.at[core, first], leave, arrive)
        for step in (1, 3, 2):
            part = final.at[core, (first + 4 - step) % 4]
            wait(part, home_arrives[step - 1])
            send(other, part, part, leave, arrive)
        ends.append((final.at[1 - core], leave))
        return arrive

    def unpack(final, which, target):
        for tile in range(HALF):
            place, at = tile // PART, tile % PART
            row = pl.ds(pl.multiple_of(which * HALF_ROWS + tile % 18 * 16, 16), 16)
            lane = tile // 18 * 128
            target[row, lane : lane + 128] = final[which, place, at // PIECE, at % PIECE]

    wait(*out_copies)
    out_total[0:PIECE] = out_grid[second] + out_second[0] + out_second[1] + out_second[2]
    out_total[PIECE:] = jnp.zeros((16 - PIECE, 16, 128), f32)
    out_thirds = send_third(out_total, out_third)

    wait(value_second, value_arrive)
    value_total[0:SLOTS] = value_grid[second] + value_second[0] + value_second[1] + value_second[2]
    value_total[SLOTS:] = jnp.zeros((16 - SLOTS, 16, 128), f32)
    value_thirds = send_third(value_total, value_third)

    _, *out_back = send_back(out_total, out_third, out_thirds, out_owned, out_all)

    small_sum, *value_back = send_back(value_total, value_third, value_thirds, value_owned, value_all)
    small_owned[...] = small_sum
    mine = small_slots.at[second]
    small_leave, small_arrive = new_sem(), new_sem()

    @pl.when(z == OWNERS)
    def _():
        small_slots[second] = small_sum
        for step in z_order():
            send(third_peer(step)[0], small_owned, mine, small_leave, small_arrive)

    end_back(out_all, *out_back)
    out_spread, *out_homes = send_spread(out_all, out_final)

    end_back(value_all, *value_back)
    value_spread, *value_homes = send_spread(value_all, value_final)

    @pl.when(z == OWNERS)
    def _():
        wait(value_total.at[0 : 7 * OWNED], small_leave)

    @pl.when(z != OWNERS)
    def _():
        wait(mine, small_arrive)

    small_spread = send_all(
        [(second_peer(step)[0], mine, mine) for step in (2, 1, 3)], small_slots.at[0:3]
    )
    forward_spread(out_final, out_spread, *out_homes)
    forward_spread(value_final, value_spread, *value_homes)

    wait(*visit_copies)
    caption_total = backs[0] + backs_got[0] + backs_got[1]
    caption_out[...] = (
        caption_total - own_unit * jnp.sum(own_unit * caption_total, axis=-1, keepdims=True)
    ) / own_length
    out_cross = forward_homes(out_final, out_homes[1])

    wait(*small_spread)
    small = []
    for tile in range(SMALL_TILES):
        both = small_slots[tile // 2, tile % 2]
        small += [both[0:8], both[8:16]]
    probe_out[...] = jnp.sum(jnp.concatenate(small[9:], axis=1)[:, :ROWS], axis=0, keepdims=True)
    patch_sum = jnp.concatenate(small[:9], axis=1) * (1.0 / math.sqrt(HEAD_DIM))
    probe_columns = probe.T
    for pair in range(4):
        parts = []
        for head in (2 * pair, 2 * pair + 1):
            column = probe_columns[head * HEAD_DIM : head * HEAD_DIM + HEAD_DIM, head : head + 1]
            parts.append(column * patch_sum[head : head + 1])
        key_out[pair * 144 : pair * 144 + 144, :] = jnp.concatenate(parts, axis=0).astype(bf16)
    value_cross = forward_homes(value_final, value_homes[1])

    unpack(out_final, core, out_out)
    wait(out_final.at[1 - core], out_cross)
    unpack(out_final, 1 - core, out_out)
    unpack(value_final, core, value_out)
    wait(value_final.at[1 - core], value_cross)
    unpack(value_final, 1 - core, value_out)
    for end in ends:
        wait(*end)


def finish_kernel(*refs):
    count = len(refs) // 2
    sources, targets, sem = refs[:count], refs[count : 2 * count], refs[2 * count]
    copies = [
        pltpu.make_async_copy(source, target, sem.at[slot])
        for slot, (source, target) in enumerate(zip(sources, targets))
    ]
    for copy in copies:
        copy.start()
    for copy in copies:
        copy.wait()


def in_hbm(array):
    return pltpu.with_memory_space_constraint(array, pltpu.HBM)


def on_device(
    patches, captions, probe_query, key_weight, value_weight, out_weight, logit_scale, logit_bias
):
    f32, bf16 = jnp.float32, jnp.bfloat16
    vmem = pl.BlockSpec(memory_space=pltpu.VMEM)
    smem = pl.BlockSpec(memory_space=pltpu.SMEM)
    hbm = pl.BlockSpec(memory_space=pltpu.HBM)
    dma = pltpu.SemaphoreType.DMA
    shapes = (
        jax.ShapeDtypeStruct((IMG_DEV, D), f32),
        jax.ShapeDtypeStruct((1, ROWS), f32),
        jax.ShapeDtypeStruct((ROWS, D), bf16),
        jax.ShapeDtypeStruct((ROWS, D), bf16),
        jax.ShapeDtypeStruct((ROWS, D), bf16),
    )
    results = pl.pallas_call(
        whole_kernel,
        out_shape=shapes,
        in_specs=[smem, smem, hbm, hbm, hbm, hbm, hbm, hbm],
        out_specs=[vmem] * 5,
        scratch_shapes=[
            pltpu.VMEM((FLAT, D), bf16),
            pltpu.VMEM((IMG_DEV, D), bf16),
            pltpu.VMEM((ROWS,), bf16),
            pltpu.VMEM((VALUE_AT + ROWS, D), bf16),
            pltpu.VMEM((ROWS, D), bf16),
            pltpu.VMEM((FLAT, ROWS), bf16),
            pltpu.VMEM((FLAT, ROWS), bf16),
            pltpu.VMEM((64, PATCHES), f32),
            pltpu.VMEM((64, PATCHES), f32),
            pltpu.VMEM((3, 8, D), f32),
            pltpu.VMEM((3, 8, D), f32),
            pltpu.VMEM((2, 8, D), f32),
            pltpu.VMEM((ROWS, 8), f32),
            pltpu.VMEM((16, D), f32),
            pltpu.VMEM((16, D), bf16),
            pltpu.VMEM((HALF_ROWS + 16, FLAT), bf16),
            pltpu.VMEM((HALF_ROWS, FLAT), bf16),
            pltpu.VMEM((16, FLAT), bf16),
            pltpu.VMEM((8, WIDE), f32),
            pltpu.VMEM((LIST, 16, 128), bf16),
            pltpu.VMEM((LIST, 16, 128), bf16),
            pltpu.VMEM((LIST, 16, 128), f32),
            pltpu.VMEM((4, 2, 16, D), bf16),
            pltpu.VMEM((16, D), bf16),
            pltpu.VMEM((8, WIDE), f32),
            pltpu.VMEM((8, WIDE), f32),
            pltpu.VMEM((3, 8, WIDE), f32),
            pltpu.VMEM((ROWS, 64), f32),
            pltpu.VMEM((LIST, 16, 128), f32),
            pltpu.VMEM((12, PIECE, 16, 128), bf16),
            pltpu.VMEM((12, PIECE, 16, 128), bf16),
            pltpu.VMEM((4, SLOTS, 16, 128), f32),
            pltpu.VMEM((3, SLOTS, 16, 128), f32),
            pltpu.VMEM((16, 16, 128), f32),
            pltpu.VMEM((7, OWNED, 16, 128), f32),
            pltpu.VMEM((OWNED, 16, 128), bf16),
            pltpu.VMEM((16, 16, 128), bf16),
            pltpu.VMEM((OWNED, 16, 128), f32),
            pltpu.VMEM((4, OWNED, 16, 128), f32),
            pltpu.VMEM((2, 4, 4, PIECE, 16, 128), bf16),
            pltpu.VMEM((4, PIECE, 16, 128), f32),
            pltpu.VMEM((3, PIECE, 16, 128), f32),
            pltpu.VMEM((16, 16, 128), f32),
            pltpu.VMEM((7, OWNED, 16, 128), f32),
            pltpu.VMEM((OWNED, 16, 128), bf16),
            pltpu.VMEM((16, 16, 128), bf16),
            pltpu.VMEM((2, 4, 4, PIECE, 16, 128), bf16),
            dma((9,)),
            dma((58,)),
        ],
        compiler_params=pltpu.CompilerParams(
            collective_id=0, has_side_effects=True, vmem_limit_bytes=40 * 1024 * 1024
        ),
        name="whole",
    )(
        logit_scale,
        logit_bias,
        in_hbm(patches.reshape(FLAT, D)),
        in_hbm(captions),
        in_hbm(probe_query),
        in_hbm(key_weight.T),
        in_hbm(value_weight.T),
        in_hbm(out_weight),
    )
    caption_grad, probe_grad, key_turned, value_turned, out_grad = pl.pallas_call(
        finish_kernel,
        out_shape=shapes,
        in_specs=[vmem] * 5,
        out_specs=[hbm] * 5,
        scratch_shapes=[dma((5,))],
        compiler_params=pltpu.CompilerParams(vmem_limit_bytes=8 * 1024 * 1024),
        name="finish",
    )(*results)
    return (caption_grad, probe_grad.reshape(ROWS), key_turned.T, value_turned.T, out_grad)


def solution(mesh):
    placed = (P("dp", None, None), P("dp", None), P(), P(), P(), P(), P(), P())
    return jax.shard_map(
        on_device,
        mesh=mesh,
        in_specs=placed,
        out_specs=(P("dp", None), P(), P(), P(), P()),
        check_vma=False,
    )
```

```python
import math

import jax
import jax.numpy as jnp
from jax import lax
from jax.experimental import pallas as pl
from jax.experimental.pallas import tpu as pltpu
from jax.sharding import PartitionSpec as P

D = 1152
HEADS = 8
HEAD_DIM = 72
PATCHES = 256
IMG_DEV = 8
ROWS = HEADS * HEAD_DIM
FLAT = IMG_DEV * PATCHES
CHUNK = 512
VALUE_AT = 640

MESH = pl.DeviceIdType.MESH
HALF = 162
HALF_ROWS = 288
PART = 41
PIECE = 11
LIST = 168
OWNED = 2
OWNERS = 6
SLOTS = 14
SMALL_AT = 12
WIDE = 1280
SMALL_TILES = WIDE // 256

norm_epsilon = 1e-06


def normalize(rows):
    length = jnp.sqrt(jnp.sum(rows * rows, axis=-1, keepdims=True) + norm_epsilon)
    return (rows / length, length)


def dot(left, right, left_dim=1, right_dim=0, precision=None):
    dims = (((left_dim,), (right_dim,)), ((), ()))
    return lax.dot_general(left, right, dims, precision=precision, preferred_element_type=jnp.float32)


def split_low(values):
    high = values.astype(jnp.bfloat16).astype(jnp.float32)
    return jnp.concatenate([high, values - high], axis=0).astype(jnp.bfloat16)


def head_mask():
    head = lax.broadcasted_iota(jnp.int32, (HEADS, ROWS), 0) * HEAD_DIM
    column = lax.broadcasted_iota(jnp.int32, (HEADS, ROWS), 1)
    return (column >= head) & (column < head + HEAD_DIM)


def probe_rows(probe_ref, own_head):
    row = probe_ref[...].astype(jnp.float32).reshape(1, ROWS)
    return jnp.where(own_head, jnp.broadcast_to(row, (HEADS, ROWS)), 0.0)


def whole_kernel(
    scale_ref,
    bias_ref,
    patches_ref,
    captions_ref,
    probe_ref,
    key_ref,
    value_ref,
    out_ref,
    caption_out,
    probe_out,
    key_out,
    value_out,
    out_out,
    x_all,
    captions,
    probe_row,
    weights,
    out_weight,
    keys,
    values,
    scores,
    attention,
    units,
    backs,
    backs_got,
    turned,
    rows_wide,
    rows_own,
    away_rows,
    home_rows,
    score_rows,
    small_own,
    value_send,
    value_got,
    value_own,
    rows_all,
    rows_got,
    small_got,
    small_pair,
    small_all,
    pools,
    out_own,
    first_send,
    first_got,
    value_grid,
    value_second,
    value_total,
    value_third,
    value_owned,
    value_all,
    small_owned,
    small_slots,
    value_final,
    out_grid,
    out_second,
    out_total,
    out_leaving,
    out_third,
    out_owned,
    out_all,
    out_final,
    load_sem,
    link_sem,
):
    f32, bf16 = jnp.float32, jnp.bfloat16
    highest = lax.Precision.HIGHEST
    me = lax.axis_index("dp")
    core, x, y, z = me % 2, (me // 2) % 4, (me // 8) % 4, me // 32
    first = x + (y - x) * core
    second = y + (x - y) * core

    def device_at(at_z, at_first, at_second, at_core):
        at_x = at_first + (at_second - at_first) * core
        at_y = at_second + (at_first - at_second) * core
        return ((at_z * 4 + at_y) * 4 + at_x) * 2 + at_core

    other = device_at(z, first, second, 1 - core)

    def first_peer(step):
        place = (first + step) % 4
        return device_at(z, place, second, core), place

    def second_peer(step):
        place = (second + step) % 4
        return device_at(z, first, place, core), place

    def third_peer(step):
        place = (z + step) % 8
        return device_at(place, first, second, core), place

    peers = [other]
    peers += [first_peer(step)[0] for step in (1, 2, 3)]
    peers += [second_peer(step)[0] for step in (1, 2, 3)]
    peers += [third_peer(step)[0] for step in range(1, 8)]
    peers += [(me + step) % 256 for step in (1, 2, 254, 255)]
    barrier = pltpu.get_barrier_semaphore()
    for peer in peers:
        pl.semaphore_signal(barrier, inc=1, device_id=(peer,), device_id_type=MESH)

    def load(source, target, slot):
        return pltpu.make_async_copy(source, target, load_sem.at[slot])

    def load_rows(slot):
        part = pl.ds(pl.multiple_of(slot * CHUNK, CHUNK), CHUNK)
        return load(patches_ref.at[part], x_all.at[part], slot)

    load(probe_ref, probe_row, 8).start()
    load(key_ref, weights.at[0:ROWS], 4).start()
    load(value_ref, weights.at[VALUE_AT : VALUE_AT + ROWS], 5).start()
    load_rows(0).start()
    load(captions_ref, captions, 7).start()
    for slot in (1, 2, 3):
        load_rows(slot).start()
    load(out_ref, out_weight, 6).start()
    weights[ROWS:VALUE_AT, :] = jnp.zeros((VALUE_AT - ROWS, D), bf16)

    used = []
    ends = []

    def new_sem():
        used.append(None)
        return link_sem.at[len(used) - 1]

    def send(device, source, target, leave, arrive):
        pltpu.make_async_remote_copy(
            src_ref=source,
            dst_ref=target,
            send_sem=leave,
            recv_sem=arrive,
            device_id=(device,),
            device_id_type=MESH,
        ).start()

    def wait(bytes_of, sem):
        pltpu.make_async_copy(bytes_of, bytes_of, sem).wait()

    def send_all(copies, bytes_of):
        leave, arrive = new_sem(), new_sem()
        for device, source, target in copies:
            send(device, source, target, leave, arrive)
        ends.append((bytes_of, leave))
        return bytes_of, arrive

    own_head = head_mask()
    load(probe_ref, probe_row, 8).wait()
    probe = probe_rows(probe_row, own_head)
    probe_low = probe.astype(bf16)

    def project(step, unused):
        load_rows(step).wait()
        part = pl.ds(pl.multiple_of(step * CHUNK, CHUNK), CHUNK)
        both = dot(x_all[part, :], weights[...], 1, 1)
        key_rows = both[:, :ROWS].astype(bf16)
        keys[part, :] = key_rows
        values[part, :] = both[:, VALUE_AT:].astype(bf16)
        score = dot(probe_low, key_rows, 1, 1)
        at = pl.multiple_of(step * 16, 16)
        scores[pl.ds(at, 8), :] = score[:, :PATCHES]
        scores[pl.ds(at + 8, 8), :] = score[:, PATCHES:]
        return unused

    load(key_ref, weights.at[0:ROWS], 4).wait()
    load(value_ref, weights.at[VALUE_AT : VALUE_AT + ROWS], 5).wait()
    lax.fori_loop(0, 2, project, 0)
    load(captions_ref, captions, 7).wait()
    own_unit, own_length = normalize(captions[...].astype(f32))
    units[0] = own_unit
    pl.semaphore_wait(barrier, len(peers))
    unit_copies = send_all(
        [((me + step) % 256, units.at[0], units.at[step]) for step in (1, 2)], units.at[1:3]
    )
    lax.fori_loop(2, 4, project, 0)

    score = scores[...] * (1.0 / math.sqrt(HEAD_DIM))
    raised = jnp.exp(score - jnp.max(score, axis=-1, keepdims=True))
    attend = raised / jnp.sum(raised, axis=-1, keepdims=True)
    attention[...] = attend
    pooled = []
    for image in range(IMG_DEV):
        weights = attend[image * 8 : image * 8 + 8].astype(bf16)
        mixed = dot(weights, values[image * PATCHES : (image + 1) * PATCHES, :])
        pooled.append(jnp.sum(jnp.where(own_head, mixed, 0.0), axis=0, keepdims=True))
    pooled = jnp.concatenate(pooled, axis=0)
    load(out_ref, out_weight, 6).wait()
    embedding = dot(pooled.astype(bf16), out_weight[...])
    image_unit, image_length = normalize(embedding)

    wait(*unit_copies)
    caption_units = units[...].reshape(24, D)
    scale, bias = scale_ref[0], bias_ref[0]
    logits = scale * dot(image_unit, caption_units, 1, 1, highest) + bias
    same = lax.broadcasted_iota(jnp.int32, (8, 24), 0) == lax.broadcasted_iota(jnp.int32, (8, 24), 1)
    slope = jax.nn.sigmoid(logits) - jnp.where(same, 1.0, 0.0)
    image_total = scale * dot(slope, caption_units, 1, 0, highest)
    embedding_grad = (
        image_total - image_unit * jnp.sum(image_unit * image_total, axis=-1, keepdims=True)
    ) / image_length
    rows_wide[...] = jnp.zeros((16, D), f32)
    rows_wide[0:8, :] = embedding_grad
    rows_wide[8:16, 0:ROWS] = pooled
    rows_own[...] = rows_wide[...].astype(bf16)
    rows_copy = send_all([(other, rows_own, rows_got)], rows_got)
    backs[...] = (scale * dot(slope, image_unit, 0, 0, highest)).reshape(3, 8, D)
    visit_copies = send_all(
        [
            ((me + 256 - step) % 256, backs.at[step], backs_got.at[step - 1])
            for step in (1, 2)
        ],
        backs_got,
    )

    grad_low = embedding_grad.astype(bf16)
    pooled_grad = dot(grad_low, out_weight[...], 1, 1)
    turned[...] = dot(out_weight[...], grad_low, 1, 1)
    attention_grad = []
    for image in range(IMG_DEV):
        spread_grad = jnp.where(
            own_head, jnp.broadcast_to(pooled_grad[image : image + 1], (HEADS, ROWS)), 0.0
        )
        both = dot(split_low(spread_grad), values[image * PATCHES : (image + 1) * PATCHES, :], 1, 1)
        attention_grad.append(both[0:8] + both[8:16])
    attention_grad = jnp.concatenate(attention_grad, axis=0)
    score_grad = attend * (
        attention_grad - jnp.sum(attend * attention_grad, axis=-1, keepdims=True)
    )

    def value_rows_grad(start, target):
        for image in range(IMG_DEV):
            for pair in range(2):
                parts = []
                for place in (2 * pair, 2 * pair + 1):
                    at = start + place
                    grads = turned[pl.ds(pl.multiple_of(at * HEAD_DIM, 8), HEAD_DIM), image : image + 1]
                    parts.append(grads * attention[pl.ds(image * 8 + at, 1), :])
                target[pair * 144 : pair * 144 + 144, image * PATCHES : (image + 1) * PATCHES] = (
                    jnp.concatenate(parts, axis=0).astype(bf16)
                )

    value_rows_grad((1 - core) * 4, away_rows)
    for image in range(IMG_DEV):
        part = score_grad[image * 8 : image * 8 + 8]
        lanes = slice(image * PATCHES, (image + 1) * PATCHES)
        away_rows[HALF_ROWS : HALF_ROWS + 16, lanes] = jnp.concatenate(
            [part, jnp.zeros((8, PATCHES), f32)], axis=0
        ).astype(bf16)
        score_rows[:, lanes] = split_low(part)

    wait(*rows_copy)
    rows_all[0, 0] = rows_own[...]
    rows_all[0, 1] = rows_got[...]
    row_gathers = send_all(
        [(first_peer(step)[0], rows_all.at[0], rows_all.at[step]) for step in (2, 1, 3)],
        rows_all.at[1:4],
    )

    value_send[HALF:] = jnp.zeros((LIST - HALF, 16, 128), bf16)
    pair_leave, pair_arrive = new_sem(), new_sem()
    ends.append((value_send, pair_leave))
    for block in range(5):
        lanes = slice(block * 256, min(block * 256 + 256, D))
        term = dot(away_rows[...], x_all[:, lanes])
        for tile in range(block * 36, min(block * 36 + 36, HALF)):
            row, lane = tile % 18 * 16, tile // 18 * 128 - block * 256
            value_send[tile] = term[row : row + 16, lane : lane + 128].astype(bf16)
        small_own[:, lanes] = term[HALF_ROWS : HALF_ROWS + 8]
        if block > 0:
            start = (block - 1) * PART
            part = slice(start, start + PART if block < 4 else LIST)
            send(other, value_send.at[part], value_got.at[part], pair_leave, pair_arrive)
    probe_part = dot(score_rows[...], keys[...])
    probe_part = jnp.where(own_head, probe_part[0:8] + probe_part[8:16], 0.0)
    probe_part = jnp.sum(probe_part, axis=0, keepdims=True) * (1.0 / math.sqrt(HEAD_DIM))
    small_own[:, D:WIDE] = jnp.zeros((8, WIDE - D), f32)
    for row in range(5):
        count = min(128, ROWS - row * 128)
        small_own[row : row + 1, D : D + count] = probe_part[:, row * 128 : row * 128 + count]
    small_copy = send_all([(other, small_own, small_got)], small_got)

    value_rows_grad(core * 4, home_rows)
    for block in range(5):
        lanes = slice(block * 256, min(block * 256 + 256, D))
        term = dot(home_rows[...], x_all[:, lanes])
        for tile in range(block * 36, min(block * 36 + 36, HALF)):
            row, lane = tile % 18 * 16, tile // 18 * 128 - block * 256
            value_own[tile] = term[row : row + 16, lane : lane + 128]
    value_own[HALF:] = jnp.zeros((LIST - HALF, 16, 128), f32)

    def piece_at(place, piece):
        return pl.ds(place * PART + piece * PIECE, PIECE)

    wait(value_got, pair_arrive)
    first_copies = []
    for ahead in (2, 1, 3, 0):
        piece = (second + ahead) % 4
        copies = []
        for step in (2, 1, 3):
            device, place = first_peer(step)
            slot = ahead * 3 + step - 1
            part = piece_at(place, piece)
            first_send[slot] = (value_own[part] + value_got[part].astype(f32)).astype(bf16)
            copies.append((device, first_send.at[slot], first_got.at[slot]))
        first_copies.append((ahead, send_all(copies, first_got.at[ahead * 3 : ahead * 3 + 3])))

    wait(*small_copy)
    small_pair[...] = small_own[...] + small_got[...]
    small_gathers = send_all(
        [(first_peer(step)[0], small_pair, small_all.at[step - 1]) for step in (2, 1, 3)], small_all
    )
    wait(*row_gathers)
    rows = rows_all[...].astype(f32).reshape(8, 16, D)
    embedding_grads = rows[:, :8].reshape(64, D).astype(bf16)
    pools[...] = rows[:, 8:, :ROWS].reshape(64, ROWS).T
    for block in range(3):
        at = pl.multiple_of(core * HALF_ROWS + block * 96, 32)
        term = dot(pools[pl.ds(at, 96), :].astype(bf16), embedding_grads)
        for row in range(6):
            for lane in range(9):
                out_own[lane * 18 + block * 6 + row] = term[
                    row * 16 : row * 16 + 16, lane * 128 : lane * 128 + 128
                ]
    out_own[HALF:] = jnp.zeros((LIST - HALF, 16, 128), f32)

    for piece in range(4):
        out_grid[piece] = out_own[piece_at(first, piece)].astype(bf16)
    out_copies = send_all(
        [
            (second_peer(step)[0], out_grid.at[second_peer(step)[1]], out_second.at[step - 1])
            for step in (2, 1, 3)
        ],
        out_second,
    )

    wait(*small_gathers)
    small = small_pair[...] + small_all[0] + small_all[1] + small_all[2]
    value_grid[:, PIECE:] = jnp.zeros((4, SLOTS - PIECE, 16, 128), f32)
    for tile in range(SMALL_TILES):
        at = (tile // 2, SMALL_AT + tile % 2)
        value_grid[at[0], at[1], 0:8] = small[:, tile * 256 : tile * 256 + 128]
        value_grid[at[0], at[1], 8:16] = small[:, tile * 256 + 128 : tile * 256 + 256]
    value_leave, value_arrive = new_sem(), new_sem()
    for ahead, copies in first_copies:
        wait(*copies)
        device, piece = second_peer(ahead)
        part = piece_at(first, piece)
        term = value_own[part] + value_got[part].astype(f32)
        for step in (1, 2, 3):
            term = term + first_got[ahead * 3 + step - 1].astype(f32)
        value_grid[piece, 0:PIECE] = term
        if ahead > 0:
            send(device, value_grid.at[piece], value_second.at[ahead - 1], value_leave, value_arrive)
    ends.append((value_second, value_leave))

    def z_order():
        return (4, 3, 5, 2, 6, 1, 7)

    def send_third(total, got, owners):
        leave, arrive = new_sem(), new_sem()
        for step in z_order():
            device, place = third_peer(step)

            @pl.when(place < owners)
            def _():
                source = total.at[pl.ds(place * OWNED, OWNED)]
                send(device, source, got.at[step - 1], leave, arrive)

        return leave, arrive

    def send_back(total, got, leave, arrive, owners, owned, every):
        @pl.when(z < owners)
        def _():
            wait(got, arrive)
            wait(got.at[0 : owners - 1], leave)

        @pl.when(z >= owners)
        def _():
            wait(got.at[0:owners], leave)

        leave, arrive = new_sem(), new_sem()
        mine = pl.ds(z * OWNED, OWNED)

        @pl.when(z < owners)
        def _():
            result = total[mine]
            for slot in range(7):
                result = result + got[slot].astype(f32)
            total[mine] = result

        @pl.when(z < OWNERS)
        def _():
            result = total[mine].astype(bf16)
            owned[...] = result
            every[mine] = result
            for step in z_order():
                send(third_peer(step)[0], owned, every.at[mine], leave, arrive)

        return leave, arrive

    def end_back(every, leave, arrive):
        @pl.when(z < OWNERS)
        def _():
            wait(every.at[0 : (OWNERS - 1) * OWNED], arrive)
            wait(every.at[0 : 7 * OWNED], leave)

        @pl.when(z >= OWNERS)
        def _():
            wait(every.at[0 : OWNERS * OWNED], arrive)

    def send_home(part, final, leave, arrives):
        piece = final.at[core, first, part]
        for step in (2, 1, 3):
            send(first_peer(step)[0], piece, piece, leave, arrives[step - 1])

    def send_spread(every, final):
        final[core, first, second] = every[0:PIECE]
        piece = final.at[core, first, second]
        leave, arrives = new_sem(), [new_sem() for _ in range(3)]
        for step in (2, 1, 3):
            send(second_peer(step)[0], every.at[0:PIECE], piece, leave, arrives[step - 1])
        ends.append((final.at[core, first, 0:3], leave))
        home_leave, home_arrives = new_sem(), [new_sem() for _ in range(3)]
        send_home(second, final, home_leave, home_arrives)
        ends.append((final.at[core, 0:3], home_leave))
        return arrives, home_leave, home_arrives

    def forward_spread(final, arrives, home_leave, home_arrives):
        for step in (1, 3, 2):
            place = (second + 4 - step) % 4
            wait(final.at[core, first, place], arrives[step - 1])
            send_home(place, final, home_leave, home_arrives)

    def forward_homes(final, home_arrives):
        leave, arrive = new_sem(), new_sem()
        send(other, final.at[core, first], final.at[core, first], leave, arrive)
        for step in (1, 3, 2):
            part = final.at[core, (first + 4 - step) % 4]
            wait(part, home_arrives[step - 1])
            send(other, part, part, leave, arrive)
        ends.append((final.at[1 - core], leave))
        return arrive

    def unpack(final, which, target):
        for tile in range(HALF):
            place, at = tile // PART, tile % PART
            row = pl.ds(pl.multiple_of(which * HALF_ROWS + tile % 18 * 16, 16), 16)
            lane = tile // 18 * 128
            target[row, lane : lane + 128] = final[which, place, at // PIECE, at % PIECE]

    wait(*out_copies)
    out_sum = out_own[piece_at(first, second)]
    for slot in range(3):
        out_sum = out_sum + out_second[slot].astype(f32)
    out_total[0:PIECE] = out_sum
    out_total[PIECE:] = jnp.zeros((16 - PIECE, 16, 128), f32)
    out_leaving[...] = out_total[...].astype(bf16)
    out_thirds = send_third(out_leaving, out_third, OWNERS)

    wait(value_second, value_arrive)
    value_total[0:SLOTS] = value_grid[second] + value_second[0] + value_second[1] + value_second[2]
    value_total[SLOTS:] = jnp.zeros((16 - SLOTS, 16, 128), f32)
    value_thirds = send_third(value_total, value_third, OWNERS + 1)

    out_back = send_back(out_total, out_third, *out_thirds, OWNERS, out_owned, out_all)

    value_back = send_back(
        value_total, value_third, *value_thirds, OWNERS + 1, value_owned, value_all
    )
    mine = small_slots.at[second]
    small_leave, small_arrive = new_sem(), new_sem()

    @pl.when(z == OWNERS)
    def _():
        small_sum = value_total[OWNERS * OWNED : (OWNERS + 1) * OWNED]
        small_owned[...] = small_sum
        small_slots[second] = small_sum
        for step in z_order():
            send(third_peer(step)[0], small_owned, mine, small_leave, small_arrive)

    end_back(out_all, *out_back)
    out_spread, *out_homes = send_spread(out_all, out_final)

    end_back(value_all, *value_back)
    value_spread, *value_homes = send_spread(value_all, value_final)
    forward_spread(out_final, out_spread, *out_homes)

    @pl.when(z == OWNERS)
    def _():
        wait(value_third, small_leave)

    @pl.when(z != OWNERS)
    def _():
        wait(mine, small_arrive)

    small_spread = send_all(
        [(second_peer(step)[0], mine, mine) for step in (2, 1, 3)], small_slots.at[0:3]
    )
    forward_spread(value_final, value_spread, *value_homes)

    wait(*visit_copies)
    caption_total = backs[0] + backs_got[0] + backs_got[1]
    caption_out[...] = (
        caption_total - own_unit * jnp.sum(own_unit * caption_total, axis=-1, keepdims=True)
    ) / own_length
    out_cross = forward_homes(out_final, out_homes[1])

    wait(*small_spread)
    small = []
    for tile in range(SMALL_TILES):
        both = small_slots[tile // 2, tile % 2]
        small += [both[0:8], both[8:16]]
    probe_sum = jnp.concatenate([small[9][row : row + 1] for row in range(5)], axis=1)
    probe_out[...] = jnp.sum(probe_sum[:, :ROWS], axis=0)
    patch_sum = jnp.concatenate(small[:9], axis=1) * (1.0 / math.sqrt(HEAD_DIM))
    probe_columns = probe.T
    for pair in range(4):
        parts = []
        for head in (2 * pair, 2 * pair + 1):
            column = probe_columns[head * HEAD_DIM : head * HEAD_DIM + HEAD_DIM, head : head + 1]
            parts.append(column * patch_sum[head : head + 1])
        key_out[pair * 144 : pair * 144 + 144, :] = jnp.concatenate(parts, axis=0).astype(bf16)
    value_cross = forward_homes(value_final, value_homes[1])

    unpack(out_final, core, out_out)
    wait(out_final.at[1 - core], out_cross)
    unpack(out_final, 1 - core, out_out)
    unpack(value_final, core, value_out)
    wait(value_final.at[1 - core], value_cross)
    unpack(value_final, 1 - core, value_out)
    for end in ends:
        wait(*end)


def finish_kernel(*refs):
    count = len(refs) // 2
    sources, targets, sem = refs[:count], refs[count : 2 * count], refs[2 * count]
    copies = [
        pltpu.make_async_copy(source, target, sem.at[slot])
        for slot, (source, target) in enumerate(zip(sources, targets))
    ]
    for copy in copies:
        copy.start()
    for copy in copies:
        copy.wait()


def in_hbm(array):
    return pltpu.with_memory_space_constraint(array, pltpu.HBM)


def on_device(
    patches, captions, probe_query, key_weight, value_weight, out_weight, logit_scale, logit_bias
):
    f32, bf16 = jnp.float32, jnp.bfloat16
    vmem = pl.BlockSpec(memory_space=pltpu.VMEM)
    smem = pl.BlockSpec(memory_space=pltpu.SMEM)
    hbm = pl.BlockSpec(memory_space=pltpu.HBM)
    dma = pltpu.SemaphoreType.DMA
    shapes = (
        jax.ShapeDtypeStruct((IMG_DEV, D), f32),
        jax.ShapeDtypeStruct((ROWS,), f32),
        jax.ShapeDtypeStruct((ROWS, D), bf16),
        jax.ShapeDtypeStruct((ROWS, D), bf16),
        jax.ShapeDtypeStruct((ROWS, D), bf16),
    )
    results = pl.pallas_call(
        whole_kernel,
        out_shape=shapes,
        in_specs=[smem, smem, hbm, hbm, hbm, hbm, hbm, hbm],
        out_specs=[vmem] * 5,
        scratch_shapes=[
            pltpu.VMEM((FLAT, D), bf16),
            pltpu.VMEM((IMG_DEV, D), bf16),
            pltpu.VMEM((ROWS,), bf16),
            pltpu.VMEM((VALUE_AT + ROWS, D), bf16),
            pltpu.VMEM((ROWS, D), bf16),
            pltpu.VMEM((FLAT, ROWS), bf16),
            pltpu.VMEM((FLAT, ROWS), bf16),
            pltpu.VMEM((64, PATCHES), f32),
            pltpu.VMEM((64, PATCHES), f32),
            pltpu.VMEM((3, 8, D), f32),
            pltpu.VMEM((3, 8, D), f32),
            pltpu.VMEM((2, 8, D), f32),
            pltpu.VMEM((ROWS, 8), f32),
            pltpu.VMEM((16, D), f32),
            pltpu.VMEM((16, D), bf16),
            pltpu.VMEM((HALF_ROWS + 16, FLAT), bf16),
            pltpu.VMEM((HALF_ROWS, FLAT), bf16),
            pltpu.VMEM((16, FLAT), bf16),
            pltpu.VMEM((8, WIDE), f32),
            pltpu.VMEM((LIST, 16, 128), bf16),
            pltpu.VMEM((LIST, 16, 128), bf16),
            pltpu.VMEM((LIST, 16, 128), f32),
            pltpu.VMEM((4, 2, 16, D), bf16),
            pltpu.VMEM((16, D), bf16),
            pltpu.VMEM((8, WIDE), f32),
            pltpu.VMEM((8, WIDE), f32),
            pltpu.VMEM((3, 8, WIDE), f32),
            pltpu.VMEM((ROWS, 64), f32),
            pltpu.VMEM((LIST, 16, 128), f32),
            pltpu.VMEM((12, PIECE, 16, 128), bf16),
            pltpu.VMEM((12, PIECE, 16, 128), bf16),
            pltpu.VMEM((4, SLOTS, 16, 128), f32),
            pltpu.VMEM((3, SLOTS, 16, 128), f32),
            pltpu.VMEM((16, 16, 128), f32),
            pltpu.VMEM((7, OWNED, 16, 128), f32),
            pltpu.VMEM((OWNED, 16, 128), bf16),
            pltpu.VMEM((16, 16, 128), bf16),
            pltpu.VMEM((OWNED, 16, 128), f32),
            pltpu.VMEM((4, OWNED, 16, 128), f32),
            pltpu.VMEM((2, 4, 4, PIECE, 16, 128), bf16),
            pltpu.VMEM((4, PIECE, 16, 128), bf16),
            pltpu.VMEM((3, PIECE, 16, 128), bf16),
            pltpu.VMEM((16, 16, 128), f32),
            pltpu.VMEM((16, 16, 128), bf16),
            pltpu.VMEM((7, OWNED, 16, 128), bf16),
            pltpu.VMEM((OWNED, 16, 128), bf16),
            pltpu.VMEM((16, 16, 128), bf16),
            pltpu.VMEM((2, 4, 4, PIECE, 16, 128), bf16),
            dma((9,)),
            dma((58,)),
        ],
        compiler_params=pltpu.CompilerParams(
            collective_id=0, has_side_effects=True, vmem_limit_bytes=40 * 1024 * 1024
        ),
        name="whole",
    )(
        logit_scale,
        logit_bias,
        in_hbm(patches.reshape(FLAT, D)),
        in_hbm(captions),
        in_hbm(probe_query),
        in_hbm(key_weight.T),
        in_hbm(value_weight.T),
        in_hbm(out_weight),
    )
    caption_grad, probe_grad, key_turned, value_turned, out_grad = pl.pallas_call(
        finish_kernel,
        out_shape=shapes,
        in_specs=[vmem] * 5,
        out_specs=[hbm] * 5,
        scratch_shapes=[dma((5,))],
        compiler_params=pltpu.CompilerParams(vmem_limit_bytes=8 * 1024 * 1024),
        name="finish",
    )(*results)
    return (caption_grad, probe_grad, key_turned.T, value_turned.T, out_grad)


def solution(mesh):
    placed = (P("dp", None, None), P("dp", None), P(), P(), P(), P(), P(), P())
    return jax.shard_map(
        on_device,
        mesh=mesh,
        in_specs=placed,
        out_specs=(P("dp", None), P(), P(), P(), P()),
        check_vma=False,
    )
```

```python
import math

import jax
import jax.numpy as jnp
from jax import lax
from jax.experimental import pallas as pl
from jax.experimental.pallas import tpu as pltpu
from jax.sharding import PartitionSpec as P

D = 1152
HEADS = 8
HEAD_DIM = 72
PATCHES = 256
IMG_DEV = 8
ROWS = HEADS * HEAD_DIM
FLAT = IMG_DEV * PATCHES
CHUNK = 512
VALUE_AT = 640

MESH = pl.DeviceIdType.MESH
HALF = 162
HALF_ROWS = 288
PART = 41
PIECE = 11
LIST = 168
OWNED = 2
OWNERS = 6
SMALL_AT = 12
WIDE = 1280
SMALL_TILES = WIDE // 256

norm_epsilon = 1e-06


def normalize(rows):
    length = jnp.sqrt(jnp.sum(rows * rows, axis=-1, keepdims=True) + norm_epsilon)
    return (rows / length, length)


def dot(left, right, left_dim=1, right_dim=0, precision=None):
    dims = (((left_dim,), (right_dim,)), ((), ()))
    return lax.dot_general(left, right, dims, precision=precision, preferred_element_type=jnp.float32)


def split_low(values):
    high = values.astype(jnp.bfloat16).astype(jnp.float32)
    return jnp.concatenate([high, values - high], axis=0).astype(jnp.bfloat16)


def head_mask():
    head = lax.broadcasted_iota(jnp.int32, (HEADS, ROWS), 0) * HEAD_DIM
    column = lax.broadcasted_iota(jnp.int32, (HEADS, ROWS), 1)
    return (column >= head) & (column < head + HEAD_DIM)


def probe_rows(probe_ref, own_head):
    row = probe_ref[...].astype(jnp.float32).reshape(1, ROWS)
    return jnp.where(own_head, jnp.broadcast_to(row, (HEADS, ROWS)), 0.0)


def whole_kernel(
    scale_ref,
    bias_ref,
    patches_ref,
    captions_ref,
    probe_ref,
    key_ref,
    value_ref,
    out_ref,
    caption_out,
    probe_out,
    key_out,
    value_out,
    out_out,
    x_all,
    captions,
    probe_row,
    weights,
    out_weight,
    keys,
    values,
    scores,
    attention,
    units,
    backs,
    backs_got,
    turned,
    rows_wide,
    rows_own,
    away_rows,
    home_rows,
    score_rows,
    small_own,
    value_send,
    value_got,
    value_own,
    rows_all,
    rows_got,
    small_got,
    small_pair,
    small_all,
    pools,
    out_own,
    first_send,
    first_got,
    value_grid,
    value_second,
    small_grid,
    small_second,
    value_total,
    value_third,
    value_owned,
    value_all,
    small_owned,
    small_slots,
    value_final,
    out_grid,
    out_second,
    out_total,
    out_leaving,
    out_third,
    out_owned,
    out_all,
    out_final,
    load_sem,
    link_sem,
):
    f32, bf16 = jnp.float32, jnp.bfloat16
    highest = lax.Precision.HIGHEST
    me = lax.axis_index("dp")
    core, x, y, z = me % 2, (me // 2) % 4, (me // 8) % 4, me // 32
    first = x + (y - x) * core
    second = y + (x - y) * core

    def device_at(at_z, at_first, at_second, at_core):
        at_x = at_first + (at_second - at_first) * core
        at_y = at_second + (at_first - at_second) * core
        return ((at_z * 4 + at_y) * 4 + at_x) * 2 + at_core

    other = device_at(z, first, second, 1 - core)

    def first_peer(step):
        place = (first + step) % 4
        return device_at(z, place, second, core), place

    def second_peer(step):
        place = (second + step) % 4
        return device_at(z, first, place, core), place

    def third_peer(step):
        place = (z + step) % 8
        return device_at(place, first, second, core), place

    peers = [other]
    peers += [first_peer(step)[0] for step in (1, 2, 3)]
    peers += [second_peer(step)[0] for step in (1, 2, 3)]
    peers += [third_peer(step)[0] for step in range(1, 8)]
    peers += [(me + step) % 256 for step in (1, 2, 254, 255)]
    barrier = pltpu.get_barrier_semaphore()
    for peer in peers:
        pl.semaphore_signal(barrier, inc=1, device_id=(peer,), device_id_type=MESH)

    def load(source, target, slot):
        return pltpu.make_async_copy(source, target, load_sem.at[slot])

    def load_rows(slot):
        part = pl.ds(pl.multiple_of(slot * CHUNK, CHUNK), CHUNK)
        return load(patches_ref.at[part], x_all.at[part], slot)

    load(probe_ref, probe_row, 8).start()
    load(key_ref, weights.at[0:ROWS], 4).start()
    load(value_ref, weights.at[VALUE_AT : VALUE_AT + ROWS], 5).start()
    load_rows(0).start()
    load(captions_ref, captions, 7).start()
    for slot in (1, 2, 3):
        load_rows(slot).start()
    load(out_ref, out_weight, 6).start()
    weights[ROWS:VALUE_AT, :] = jnp.zeros((VALUE_AT - ROWS, D), bf16)

    used = []
    ends = []

    def new_sem():
        used.append(None)
        return link_sem.at[len(used) - 1]

    def send(device, source, target, leave, arrive):
        pltpu.make_async_remote_copy(
            src_ref=source,
            dst_ref=target,
            send_sem=leave,
            recv_sem=arrive,
            device_id=(device,),
            device_id_type=MESH,
        ).start()

    def wait(bytes_of, sem):
        pltpu.make_async_copy(bytes_of, bytes_of, sem).wait()

    def send_all(copies, bytes_of):
        leave, arrive = new_sem(), new_sem()
        for device, source, target in copies:
            send(device, source, target, leave, arrive)
        ends.append((bytes_of, leave))
        return bytes_of, arrive

    own_head = head_mask()
    load(probe_ref, probe_row, 8).wait()
    probe = probe_rows(probe_row, own_head)
    probe_low = probe.astype(bf16)

    def project(step, unused):
        load_rows(step).wait()
        part = pl.ds(pl.multiple_of(step * CHUNK, CHUNK), CHUNK)
        both = dot(x_all[part, :], weights[...], 1, 1)
        key_rows = both[:, :ROWS].astype(bf16)
        keys[part, :] = key_rows
        values[part, :] = both[:, VALUE_AT:].astype(bf16)
        score = dot(probe_low, key_rows, 1, 1)
        at = pl.multiple_of(step * 16, 16)
        scores[pl.ds(at, 8), :] = score[:, :PATCHES]
        scores[pl.ds(at + 8, 8), :] = score[:, PATCHES:]
        return unused

    load(key_ref, weights.at[0:ROWS], 4).wait()
    load(value_ref, weights.at[VALUE_AT : VALUE_AT + ROWS], 5).wait()
    lax.fori_loop(0, 2, project, 0)
    load(captions_ref, captions, 7).wait()
    own_unit, own_length = normalize(captions[...].astype(f32))
    units[0] = own_unit
    pl.semaphore_wait(barrier, len(peers))
    unit_copies = send_all(
        [((me + step) % 256, units.at[0], units.at[step]) for step in (1, 2)], units.at[1:3]
    )
    lax.fori_loop(2, 4, project, 0)

    score = scores[...] * (1.0 / math.sqrt(HEAD_DIM))
    raised = jnp.exp(score - jnp.max(score, axis=-1, keepdims=True))
    attend = raised / jnp.sum(raised, axis=-1, keepdims=True)
    attention[...] = attend
    pooled = []
    for image in range(IMG_DEV):
        weights = attend[image * 8 : image * 8 + 8].astype(bf16)
        mixed = dot(weights, values[image * PATCHES : (image + 1) * PATCHES, :])
        pooled.append(jnp.sum(jnp.where(own_head, mixed, 0.0), axis=0, keepdims=True))
    pooled = jnp.concatenate(pooled, axis=0)
    load(out_ref, out_weight, 6).wait()
    embedding = dot(pooled.astype(bf16), out_weight[...])
    image_unit, image_length = normalize(embedding)

    wait(*unit_copies)
    caption_units = units[...].reshape(24, D)
    scale, bias = scale_ref[0], bias_ref[0]
    logits = scale * dot(image_unit, caption_units, 1, 1, highest) + bias
    same = lax.broadcasted_iota(jnp.int32, (8, 24), 0) == lax.broadcasted_iota(jnp.int32, (8, 24), 1)
    slope = jax.nn.sigmoid(logits) - jnp.where(same, 1.0, 0.0)
    image_total = scale * dot(slope, caption_units, 1, 0, highest)
    embedding_grad = (
        image_total - image_unit * jnp.sum(image_unit * image_total, axis=-1, keepdims=True)
    ) / image_length
    rows_wide[...] = jnp.zeros((16, D), f32)
    rows_wide[0:8, :] = embedding_grad
    rows_wide[8:16, 0:ROWS] = pooled
    rows_own[...] = rows_wide[...].astype(bf16)
    rows_copy = send_all([(other, rows_own, rows_got)], rows_got)
    backs[...] = (scale * dot(slope, image_unit, 0, 0, highest)).reshape(3, 8, D)
    visit_copies = send_all(
        [
            ((me + 256 - step) % 256, backs.at[step], backs_got.at[step - 1])
            for step in (1, 2)
        ],
        backs_got,
    )

    grad_low = embedding_grad.astype(bf16)
    pooled_grad = dot(grad_low, out_weight[...], 1, 1)
    turned[...] = dot(out_weight[...], grad_low, 1, 1)
    attention_grad = []
    for image in range(IMG_DEV):
        spread_grad = jnp.where(
            own_head, jnp.broadcast_to(pooled_grad[image : image + 1], (HEADS, ROWS)), 0.0
        )
        both = dot(split_low(spread_grad), values[image * PATCHES : (image + 1) * PATCHES, :], 1, 1)
        attention_grad.append(both[0:8] + both[8:16])
    attention_grad = jnp.concatenate(attention_grad, axis=0)
    score_grad = attend * (
        attention_grad - jnp.sum(attend * attention_grad, axis=-1, keepdims=True)
    )

    def value_rows_grad(start, target):
        for image in range(IMG_DEV):
            for pair in range(2):
                parts = []
                for place in (2 * pair, 2 * pair + 1):
                    at = start + place
                    grads = turned[pl.ds(pl.multiple_of(at * HEAD_DIM, 8), HEAD_DIM), image : image + 1]
                    parts.append(grads * attention[pl.ds(image * 8 + at, 1), :])
                target[pair * 144 : pair * 144 + 144, image * PATCHES : (image + 1) * PATCHES] = (
                    jnp.concatenate(parts, axis=0).astype(bf16)
                )

    value_rows_grad((1 - core) * 4, away_rows)
    for image in range(IMG_DEV):
        part = score_grad[image * 8 : image * 8 + 8]
        lanes = slice(image * PATCHES, (image + 1) * PATCHES)
        away_rows[HALF_ROWS : HALF_ROWS + 16, lanes] = jnp.concatenate(
            [part, jnp.zeros((8, PATCHES), f32)], axis=0
        ).astype(bf16)
        score_rows[:, lanes] = split_low(part)

    wait(*rows_copy)
    rows_all[0, 0] = rows_own[...]
    rows_all[0, 1] = rows_got[...]
    row_gathers = send_all(
        [(first_peer(step)[0], rows_all.at[0], rows_all.at[step]) for step in (2, 1, 3)],
        rows_all.at[1:4],
    )

    value_send[HALF:] = jnp.zeros((LIST - HALF, 16, 128), f32)
    pair_leave, pair_arrive = new_sem(), new_sem()
    ends.append((value_send, pair_leave))
    for block in range(5):
        lanes = slice(block * 256, min(block * 256 + 256, D))
        term = dot(away_rows[...], x_all[:, lanes])
        for tile in range(block * 36, min(block * 36 + 36, HALF)):
            row, lane = tile % 18 * 16, tile // 18 * 128 - block * 256
            value_send[tile] = term[row : row + 16, lane : lane + 128]
        small_own[:, lanes] = term[HALF_ROWS : HALF_ROWS + 8]
        if block > 0:
            start = (block - 1) * PART
            part = slice(start, start + PART if block < 4 else LIST)
            send(other, value_send.at[part], value_got.at[part], pair_leave, pair_arrive)
    probe_part = dot(score_rows[...], keys[...])
    probe_part = jnp.where(own_head, probe_part[0:8] + probe_part[8:16], 0.0)
    probe_part = jnp.sum(probe_part, axis=0, keepdims=True) * (1.0 / math.sqrt(HEAD_DIM))
    small_own[:, D:WIDE] = jnp.zeros((8, WIDE - D), f32)
    for row in range(5):
        count = min(128, ROWS - row * 128)
        small_own[row : row + 1, D : D + count] = probe_part[:, row * 128 : row * 128 + count]
    small_copy = send_all([(other, small_own, small_got)], small_got)

    value_rows_grad(core * 4, home_rows)
    for block in range(5):
        lanes = slice(block * 256, min(block * 256 + 256, D))
        term = dot(home_rows[...], x_all[:, lanes])
        for tile in range(block * 36, min(block * 36 + 36, HALF)):
            row, lane = tile % 18 * 16, tile // 18 * 128 - block * 256
            value_own[tile] = term[row : row + 16, lane : lane + 128]
    value_own[HALF:] = jnp.zeros((LIST - HALF, 16, 128), f32)

    def piece_at(place, piece):
        return pl.ds(place * PART + piece * PIECE, PIECE)

    wait(value_got, pair_arrive)
    first_copies = []
    for ahead in (2, 1, 3, 0):
        piece = (second + ahead) % 4
        copies = []
        for step in (2, 1, 3):
            device, place = first_peer(step)
            slot = ahead * 3 + step - 1
            part = piece_at(place, piece)
            first_send[slot] = (value_own[part] + value_got[part]).astype(bf16)
            copies.append((device, first_send.at[slot], first_got.at[slot]))
        first_copies.append((ahead, send_all(copies, first_got.at[ahead * 3 : ahead * 3 + 3])))

    wait(*small_copy)
    small_pair[...] = small_own[...] + small_got[...]
    small_gathers = send_all(
        [(first_peer(step)[0], small_pair, small_all.at[step - 1]) for step in (2, 1, 3)], small_all
    )
    wait(*row_gathers)
    rows = rows_all[...].astype(f32).reshape(8, 16, D)
    embedding_grads = rows[:, :8].reshape(64, D).astype(bf16)
    pools[...] = rows[:, 8:, :ROWS].reshape(64, ROWS).T
    for block in range(3):
        at = pl.multiple_of(core * HALF_ROWS + block * 96, 32)
        term = dot(pools[pl.ds(at, 96), :].astype(bf16), embedding_grads)
        for row in range(6):
            for lane in range(9):
                out_own[lane * 18 + block * 6 + row] = term[
                    row * 16 : row * 16 + 16, lane * 128 : lane * 128 + 128
                ]
    out_own[HALF:] = jnp.zeros((LIST - HALF, 16, 128), f32)

    for piece in range(4):
        out_grid[piece] = out_own[piece_at(first, piece)].astype(bf16)
    out_copies = send_all(
        [
            (second_peer(step)[0], out_grid.at[second_peer(step)[1]], out_second.at[step - 1])
            for step in (2, 1, 3)
        ],
        out_second,
    )

    value_leave, value_arrive = new_sem(), new_sem()
    for ahead, copies in first_copies:
        wait(*copies)
        device, piece = second_peer(ahead)
        part = piece_at(first, piece)
        term = value_own[part] + value_got[part]
        for step in (1, 2, 3):
            term = term + first_got[ahead * 3 + step - 1].astype(f32)
        if ahead == 0:
            value_total[0:PIECE] = term
        else:
            value_grid[piece] = term.astype(bf16)
            send(device, value_grid.at[piece], value_second.at[ahead - 1], value_leave, value_arrive)
    ends.append((value_second, value_leave))
    wait(*small_gathers)
    small = small_pair[...] + small_all[0] + small_all[1] + small_all[2]
    small_grid[...] = jnp.zeros((4, OWNED, 16, 128), f32)
    for tile in range(SMALL_TILES):
        small_grid[tile // 2, tile % 2, 0:8] = small[:, tile * 256 : tile * 256 + 128]
        small_grid[tile // 2, tile % 2, 8:16] = small[:, tile * 256 + 128 : tile * 256 + 256]
    small_copies = send_all(
        [
            (second_peer(step)[0], small_grid.at[second_peer(step)[1]], small_second.at[step - 1])
            for step in (2, 1, 3)
        ],
        small_second,
    )

    def z_order():
        return (4, 3, 5, 2, 6, 1, 7)

    def send_third(total, got, owners):
        leave, arrive = new_sem(), new_sem()
        for step in z_order():
            device, place = third_peer(step)

            @pl.when(place < owners)
            def _():
                source = total.at[pl.ds(place * OWNED, OWNED)]
                send(device, source, got.at[step - 1], leave, arrive)

        return leave, arrive

    def send_back(total, got, leave, arrive, owners, owned, every):
        @pl.when(z < owners)
        def _():
            wait(got, arrive)
            wait(got.at[0 : owners - 1], leave)

        @pl.when(z >= owners)
        def _():
            wait(got.at[0:owners], leave)

        leave, arrive = new_sem(), new_sem()
        mine = pl.ds(z * OWNED, OWNED)

        @pl.when(z < owners)
        def _():
            result = total[mine]
            for slot in range(7):
                result = result + got[slot].astype(f32)
            total[mine] = result

        @pl.when(z < OWNERS)
        def _():
            result = total[mine].astype(bf16)
            owned[...] = result
            every[mine] = result
            for step in z_order():
                send(third_peer(step)[0], owned, every.at[mine], leave, arrive)

        return leave, arrive

    def end_back(every, leave, arrive):
        @pl.when(z < OWNERS)
        def _():
            wait(every.at[0 : (OWNERS - 1) * OWNED], arrive)
            wait(every.at[0 : 7 * OWNED], leave)

        @pl.when(z >= OWNERS)
        def _():
            wait(every.at[0 : OWNERS * OWNED], arrive)

    def send_home(part, final, leave, arrives):
        piece = final.at[core, first, part]
        for step in (2, 1, 3):
            send(first_peer(step)[0], piece, piece, leave, arrives[step - 1])

    def send_spread(every, final):
        final[core, first, second] = every[0:PIECE]
        piece = final.at[core, first, second]
        leave, arrives = new_sem(), [new_sem() for _ in range(3)]
        for step in (2, 1, 3):
            send(second_peer(step)[0], every.at[0:PIECE], piece, leave, arrives[step - 1])
        ends.append((final.at[core, first, 0:3], leave))
        home_leave, home_arrives = new_sem(), [new_sem() for _ in range(3)]
        send_home(second, final, home_leave, home_arrives)
        ends.append((final.at[core, 0:3], home_leave))
        return arrives, home_leave, home_arrives

    def forward_spread(final, arrives, home_leave, home_arrives):
        for step in (1, 3, 2):
            place = (second + 4 - step) % 4
            wait(final.at[core, first, place], arrives[step - 1])
            send_home(place, final, home_leave, home_arrives)

    def forward_homes(final, home_arrives):
        leave, arrive = new_sem(), new_sem()
        send(other, final.at[core, first], final.at[core, first], leave, arrive)
        for step in (1, 3, 2):
            part = final.at[core, (first + 4 - step) % 4]
            wait(part, home_arrives[step - 1])
            send(other, part, part, leave, arrive)
        ends.append((final.at[1 - core], leave))
        return arrive

    def unpack(final, which, target):
        for tile in range(HALF):
            place, at = tile // PART, tile % PART
            row = pl.ds(pl.multiple_of(which * HALF_ROWS + tile % 18 * 16, 16), 16)
            lane = tile // 18 * 128
            target[row, lane : lane + 128] = final[which, place, at // PIECE, at % PIECE]

    wait(*out_copies)
    out_sum = out_own[piece_at(first, second)]
    for slot in range(3):
        out_sum = out_sum + out_second[slot].astype(f32)
    out_total[0:PIECE] = out_sum
    out_total[PIECE:] = jnp.zeros((16 - PIECE, 16, 128), f32)
    out_leaving[...] = out_total[...].astype(bf16)
    out_thirds = send_third(out_leaving, out_third, OWNERS)

    wait(value_second, value_arrive)
    value_sum = value_total[0:PIECE]
    for slot in range(3):
        value_sum = value_sum + value_second[slot].astype(f32)
    value_total[0:PIECE] = value_sum
    wait(*small_copies)
    value_total[PIECE:] = jnp.zeros((16 - PIECE, 16, 128), f32)
    value_total[SMALL_AT : SMALL_AT + OWNED] = (
        small_grid[second] + small_second[0] + small_second[1] + small_second[2]
    )
    value_thirds = send_third(value_total, value_third, OWNERS + 1)

    out_back = send_back(out_total, out_third, *out_thirds, OWNERS, out_owned, out_all)

    value_back = send_back(
        value_total, value_third, *value_thirds, OWNERS + 1, value_owned, value_all
    )
    mine = small_slots.at[second]
    small_leave, small_arrive = new_sem(), new_sem()

    @pl.when(z == OWNERS)
    def _():
        small_sum = value_total[OWNERS * OWNED : (OWNERS + 1) * OWNED]
        small_owned[...] = small_sum
        small_slots[second] = small_sum
        for step in z_order():
            send(third_peer(step)[0], small_owned, mine, small_leave, small_arrive)

    end_back(out_all, *out_back)
    out_spread, *out_homes = send_spread(out_all, out_final)

    end_back(value_all, *value_back)
    value_spread, *value_homes = send_spread(value_all, value_final)
    forward_spread(out_final, out_spread, *out_homes)

    @pl.when(z == OWNERS)
    def _():
        wait(value_third, small_leave)

    @pl.when(z != OWNERS)
    def _():
        wait(mine, small_arrive)

    small_spread = send_all(
        [(second_peer(step)[0], mine, mine) for step in (2, 1, 3)], small_slots.at[0:3]
    )
    forward_spread(value_final, value_spread, *value_homes)

    wait(*visit_copies)
    caption_total = backs[0] + backs_got[0] + backs_got[1]
    caption_out[...] = (
        caption_total - own_unit * jnp.sum(own_unit * caption_total, axis=-1, keepdims=True)
    ) / own_length
    out_cross = forward_homes(out_final, out_homes[1])

    wait(*small_spread)
    small = []
    for tile in range(SMALL_TILES):
        both = small_slots[tile // 2, tile % 2]
        small += [both[0:8], both[8:16]]
    probe_sum = jnp.concatenate([small[9][row : row + 1] for row in range(5)], axis=1)
    probe_out[...] = jnp.sum(probe_sum[:, :ROWS], axis=0)
    patch_sum = jnp.concatenate(small[:9], axis=1) * (1.0 / math.sqrt(HEAD_DIM))
    probe_columns = probe.T
    for pair in range(4):
        parts = []
        for head in (2 * pair, 2 * pair + 1):
            column = probe_columns[head * HEAD_DIM : head * HEAD_DIM + HEAD_DIM, head : head + 1]
            parts.append(column * patch_sum[head : head + 1])
        key_out[pair * 144 : pair * 144 + 144, :] = jnp.concatenate(parts, axis=0).astype(bf16)
    value_cross = forward_homes(value_final, value_homes[1])

    unpack(out_final, core, out_out)
    wait(out_final.at[1 - core], out_cross)
    unpack(out_final, 1 - core, out_out)
    unpack(value_final, core, value_out)
    wait(value_final.at[1 - core], value_cross)
    unpack(value_final, 1 - core, value_out)
    for end in ends:
        wait(*end)


def finish_kernel(*refs):
    count = len(refs) // 2
    sources, targets, sem = refs[:count], refs[count : 2 * count], refs[2 * count]
    copies = [
        pltpu.make_async_copy(source, target, sem.at[slot])
        for slot, (source, target) in enumerate(zip(sources, targets))
    ]
    for copy in copies:
        copy.start()
    for copy in copies:
        copy.wait()


def in_hbm(array):
    return pltpu.with_memory_space_constraint(array, pltpu.HBM)


def on_device(
    patches, captions, probe_query, key_weight, value_weight, out_weight, logit_scale, logit_bias
):
    f32, bf16 = jnp.float32, jnp.bfloat16
    vmem = pl.BlockSpec(memory_space=pltpu.VMEM)
    smem = pl.BlockSpec(memory_space=pltpu.SMEM)
    hbm = pl.BlockSpec(memory_space=pltpu.HBM)
    dma = pltpu.SemaphoreType.DMA
    shapes = (
        jax.ShapeDtypeStruct((IMG_DEV, D), f32),
        jax.ShapeDtypeStruct((ROWS,), f32),
        jax.ShapeDtypeStruct((ROWS, D), bf16),
        jax.ShapeDtypeStruct((ROWS, D), bf16),
        jax.ShapeDtypeStruct((ROWS, D), bf16),
    )
    results = pl.pallas_call(
        whole_kernel,
        out_shape=shapes,
        in_specs=[smem, smem, hbm, hbm, hbm, hbm, hbm, hbm],
        out_specs=[vmem] * 5,
        scratch_shapes=[
            pltpu.VMEM((FLAT, D), bf16),
            pltpu.VMEM((IMG_DEV, D), bf16),
            pltpu.VMEM((ROWS,), bf16),
            pltpu.VMEM((VALUE_AT + ROWS, D), bf16),
            pltpu.VMEM((ROWS, D), bf16),
            pltpu.VMEM((FLAT, ROWS), bf16),
            pltpu.VMEM((FLAT, ROWS), bf16),
            pltpu.VMEM((64, PATCHES), f32),
            pltpu.VMEM((64, PATCHES), f32),
            pltpu.VMEM((3, 8, D), f32),
            pltpu.VMEM((3, 8, D), f32),
            pltpu.VMEM((2, 8, D), f32),
            pltpu.VMEM((ROWS, 8), f32),
            pltpu.VMEM((16, D), f32),
            pltpu.VMEM((16, D), bf16),
            pltpu.VMEM((HALF_ROWS + 16, FLAT), bf16),
            pltpu.VMEM((HALF_ROWS, FLAT), bf16),
            pltpu.VMEM((16, FLAT), bf16),
            pltpu.VMEM((8, WIDE), f32),
            pltpu.VMEM((LIST, 16, 128), f32),
            pltpu.VMEM((LIST, 16, 128), f32),
            pltpu.VMEM((LIST, 16, 128), f32),
            pltpu.VMEM((4, 2, 16, D), bf16),
            pltpu.VMEM((16, D), bf16),
            pltpu.VMEM((8, WIDE), f32),
            pltpu.VMEM((8, WIDE), f32),
            pltpu.VMEM((3, 8, WIDE), f32),
            pltpu.VMEM((ROWS, 64), f32),
            pltpu.VMEM((LIST, 16, 128), f32),
            pltpu.VMEM((12, PIECE, 16, 128), bf16),
            pltpu.VMEM((12, PIECE, 16, 128), bf16),
            pltpu.VMEM((4, PIECE, 16, 128), bf16),
            pltpu.VMEM((3, PIECE, 16, 128), bf16),
            pltpu.VMEM((4, OWNED, 16, 128), f32),
            pltpu.VMEM((3, OWNED, 16, 128), f32),
            pltpu.VMEM((16, 16, 128), f32),
            pltpu.VMEM((7, OWNED, 16, 128), f32),
            pltpu.VMEM((OWNED, 16, 128), bf16),
            pltpu.VMEM((16, 16, 128), bf16),
            pltpu.VMEM((OWNED, 16, 128), f32),
            pltpu.VMEM((4, OWNED, 16, 128), f32),
            pltpu.VMEM((2, 4, 4, PIECE, 16, 128), bf16),
            pltpu.VMEM((4, PIECE, 16, 128), bf16),
            pltpu.VMEM((3, PIECE, 16, 128), bf16),
            pltpu.VMEM((16, 16, 128), f32),
            pltpu.VMEM((16, 16, 128), bf16),
            pltpu.VMEM((7, OWNED, 16, 128), bf16),
            pltpu.VMEM((OWNED, 16, 128), bf16),
            pltpu.VMEM((16, 16, 128), bf16),
            pltpu.VMEM((2, 4, 4, PIECE, 16, 128), bf16),
            dma((9,)),
            dma((60,)),
        ],
        compiler_params=pltpu.CompilerParams(
            collective_id=0, has_side_effects=True, vmem_limit_bytes=40 * 1024 * 1024
        ),
        name="whole",
    )(
        logit_scale,
        logit_bias,
        in_hbm(patches.reshape(FLAT, D)),
        in_hbm(captions),
        in_hbm(probe_query),
        in_hbm(key_weight.T),
        in_hbm(value_weight.T),
        in_hbm(out_weight),
    )
    caption_grad, probe_grad, key_turned, value_turned, out_grad = pl.pallas_call(
        finish_kernel,
        out_shape=shapes,
        in_specs=[vmem] * 5,
        out_specs=[hbm] * 5,
        scratch_shapes=[dma((5,))],
        compiler_params=pltpu.CompilerParams(vmem_limit_bytes=8 * 1024 * 1024),
        name="finish",
    )(*results)
    return (caption_grad, probe_grad, key_turned.T, value_turned.T, out_grad)


def solution(mesh):
    placed = (P("dp", None, None), P("dp", None), P(), P(), P(), P(), P(), P())
    return jax.shard_map(
        on_device,
        mesh=mesh,
        in_specs=placed,
        out_specs=(P("dp", None), P(), P(), P(), P()),
        check_vma=False,
    )
```

```python
import math

import jax
import jax.numpy as jnp
from jax import lax
from jax.experimental import pallas as pl
from jax.experimental.pallas import tpu as pltpu
from jax.sharding import PartitionSpec as P

D = 1152
HEADS = 8
HEAD_DIM = 72
PATCHES = 256
IMG_DEV = 8
ROWS = HEADS * HEAD_DIM
FLAT = IMG_DEV * PATCHES
CHUNK = 512
VALUE_AT = 640

MESH = pl.DeviceIdType.MESH
HALF = 162
HALF_ROWS = 288
PART = 41
PIECE = 11
LIST = 168
OWNED = 2
OWNERS = 6
SMALL_AT = 12
WIDE = 1280
SMALL_TILES = WIDE // 256

norm_epsilon = 1e-06


def normalize(rows):
    length = jnp.sqrt(jnp.sum(rows * rows, axis=-1, keepdims=True) + norm_epsilon)
    return (rows / length, length)


def dot(left, right, left_dim=1, right_dim=0, precision=None):
    dims = (((left_dim,), (right_dim,)), ((), ()))
    return lax.dot_general(left, right, dims, precision=precision, preferred_element_type=jnp.float32)


def split_low(values):
    high = values.astype(jnp.bfloat16).astype(jnp.float32)
    return jnp.concatenate([high, values - high], axis=0).astype(jnp.bfloat16)


def head_mask():
    head = lax.broadcasted_iota(jnp.int32, (HEADS, ROWS), 0) * HEAD_DIM
    column = lax.broadcasted_iota(jnp.int32, (HEADS, ROWS), 1)
    return (column >= head) & (column < head + HEAD_DIM)


def probe_rows(probe_ref, own_head):
    row = probe_ref[...].astype(jnp.float32).reshape(1, ROWS)
    return jnp.where(own_head, jnp.broadcast_to(row, (HEADS, ROWS)), 0.0)


def whole_kernel(
    scale_ref,
    bias_ref,
    patches_ref,
    captions_ref,
    probe_ref,
    key_ref,
    value_ref,
    out_ref,
    caption_out,
    probe_out,
    key_out,
    value_out,
    out_out,
    x_all,
    captions,
    probe_row,
    weights,
    out_weight,
    keys,
    values,
    scores,
    attention,
    units,
    backs,
    backs_got,
    turned,
    rows_wide,
    rows_own,
    away_rows,
    home_rows,
    score_rows,
    small_own,
    value_send,
    value_got,
    value_own,
    rows_all,
    rows_got,
    small_got,
    small_pair,
    small_all,
    pools,
    out_own,
    first_send,
    first_got,
    value_grid,
    value_second,
    small_grid,
    small_second,
    value_total,
    value_third,
    value_owned,
    value_all,
    small_owned,
    small_slots,
    value_final,
    out_grid,
    out_second,
    out_total,
    out_leaving,
    out_third,
    out_owned,
    out_all,
    out_final,
    load_sem,
    link_sem,
):
    f32, bf16 = jnp.float32, jnp.bfloat16
    highest = lax.Precision.HIGHEST
    me = lax.axis_index("dp")
    core, x, y, z = me % 2, (me // 2) % 4, (me // 8) % 4, me // 32
    first = x + (y - x) * core
    second = y + (x - y) * core

    def device_at(at_z, at_first, at_second, at_core):
        at_x = at_first + (at_second - at_first) * core
        at_y = at_second + (at_first - at_second) * core
        return ((at_z * 4 + at_y) * 4 + at_x) * 2 + at_core

    other = device_at(z, first, second, 1 - core)

    def first_peer(step):
        place = (first + step) % 4
        return device_at(z, place, second, core), place

    def second_peer(step):
        place = (second + step) % 4
        return device_at(z, first, place, core), place

    def third_peer(step):
        place = (z + step) % 8
        return device_at(place, first, second, core), place

    peers = [other]
    peers += [first_peer(step)[0] for step in (1, 2, 3)]
    peers += [second_peer(step)[0] for step in (1, 2, 3)]
    peers += [third_peer(step)[0] for step in range(1, 8)]
    peers += [(me + step) % 256 for step in (1, 2, 254, 255)]
    barrier = pltpu.get_barrier_semaphore()
    for peer in peers:
        pl.semaphore_signal(barrier, inc=1, device_id=(peer,), device_id_type=MESH)

    def load(source, target, slot):
        return pltpu.make_async_copy(source, target, load_sem.at[slot])

    def load_rows(slot):
        part = pl.ds(pl.multiple_of(slot * CHUNK, CHUNK), CHUNK)
        return load(patches_ref.at[part], x_all.at[part], slot)

    load(probe_ref, probe_row, 8).start()
    load(key_ref, weights.at[0:ROWS], 4).start()
    load(value_ref, weights.at[VALUE_AT : VALUE_AT + ROWS], 5).start()
    load_rows(0).start()
    load(captions_ref, captions, 7).start()
    for slot in (1, 2, 3):
        load_rows(slot).start()
    load(out_ref, out_weight, 6).start()
    weights[ROWS:VALUE_AT, :] = jnp.zeros((VALUE_AT - ROWS, D), bf16)

    used = []
    ends = []

    def new_sem():
        used.append(None)
        return link_sem.at[len(used) - 1]

    def send(device, source, target, leave, arrive):
        pltpu.make_async_remote_copy(
            src_ref=source,
            dst_ref=target,
            send_sem=leave,
            recv_sem=arrive,
            device_id=(device,),
            device_id_type=MESH,
        ).start()

    def wait(bytes_of, sem):
        pltpu.make_async_copy(bytes_of, bytes_of, sem).wait()

    def send_all(copies, bytes_of):
        leave, arrive = new_sem(), new_sem()
        for device, source, target in copies:
            send(device, source, target, leave, arrive)
        ends.append((bytes_of, leave))
        return bytes_of, arrive

    own_head = head_mask()
    load(probe_ref, probe_row, 8).wait()
    probe = probe_rows(probe_row, own_head)
    probe_low = probe.astype(bf16)

    def project(step, unused):
        load_rows(step).wait()
        part = pl.ds(pl.multiple_of(step * CHUNK, CHUNK), CHUNK)
        both = dot(x_all[part, :], weights[...], 1, 1)
        key_rows = both[:, :ROWS].astype(bf16)
        keys[part, :] = key_rows
        values[part, :] = both[:, VALUE_AT:].astype(bf16)
        score = dot(probe_low, key_rows, 1, 1)
        at = pl.multiple_of(step * 16, 16)
        scores[pl.ds(at, 8), :] = score[:, :PATCHES]
        scores[pl.ds(at + 8, 8), :] = score[:, PATCHES:]
        return unused

    load(key_ref, weights.at[0:ROWS], 4).wait()
    load(value_ref, weights.at[VALUE_AT : VALUE_AT + ROWS], 5).wait()
    lax.fori_loop(0, 2, project, 0)
    load(captions_ref, captions, 7).wait()
    own_unit, own_length = normalize(captions[...].astype(f32))
    units[0] = own_unit
    pl.semaphore_wait(barrier, len(peers))
    unit_copies = send_all(
        [((me + step) % 256, units.at[0], units.at[step]) for step in (1, 2)], units.at[1:3]
    )
    lax.fori_loop(2, 4, project, 0)

    score = scores[...] * (1.0 / math.sqrt(HEAD_DIM))
    raised = jnp.exp(score - jnp.max(score, axis=-1, keepdims=True))
    attend = raised / jnp.sum(raised, axis=-1, keepdims=True)
    attention[...] = attend
    pooled = []
    for image in range(IMG_DEV):
        weights = attend[image * 8 : image * 8 + 8].astype(bf16)
        mixed = dot(weights, values[image * PATCHES : (image + 1) * PATCHES, :])
        pooled.append(jnp.sum(jnp.where(own_head, mixed, 0.0), axis=0, keepdims=True))
    pooled = jnp.concatenate(pooled, axis=0)
    load(out_ref, out_weight, 6).wait()
    embedding = dot(pooled.astype(bf16), out_weight[...])
    image_unit, image_length = normalize(embedding)

    wait(*unit_copies)
    caption_units = units[...].reshape(24, D)
    scale, bias = scale_ref[0], bias_ref[0]
    logits = scale * dot(image_unit, caption_units, 1, 1, highest) + bias
    same = lax.broadcasted_iota(jnp.int32, (8, 24), 0) == lax.broadcasted_iota(jnp.int32, (8, 24), 1)
    slope = jax.nn.sigmoid(logits) - jnp.where(same, 1.0, 0.0)
    image_total = scale * dot(slope, caption_units, 1, 0, highest)
    embedding_grad = (
        image_total - image_unit * jnp.sum(image_unit * image_total, axis=-1, keepdims=True)
    ) / image_length
    rows_wide[...] = jnp.zeros((16, D), f32)
    rows_wide[0:8, :] = embedding_grad
    rows_wide[8:16, 0:ROWS] = pooled
    rows_own[...] = rows_wide[...].astype(bf16)
    rows_copy = send_all([(other, rows_own, rows_got)], rows_got)
    backs[...] = (scale * dot(slope, image_unit, 0, 0, highest)).reshape(3, 8, D)
    visit_copies = send_all(
        [
            ((me + 256 - step) % 256, backs.at[step], backs_got.at[step - 1])
            for step in (1, 2)
        ],
        backs_got,
    )

    grad_low = embedding_grad.astype(bf16)
    pooled_grad = dot(grad_low, out_weight[...], 1, 1)
    turned[...] = dot(out_weight[...], grad_low, 1, 1)
    attention_grad = []
    for image in range(IMG_DEV):
        spread_grad = jnp.where(
            own_head, jnp.broadcast_to(pooled_grad[image : image + 1], (HEADS, ROWS)), 0.0
        )
        both = dot(split_low(spread_grad), values[image * PATCHES : (image + 1) * PATCHES, :], 1, 1)
        attention_grad.append(both[0:8] + both[8:16])
    attention_grad = jnp.concatenate(attention_grad, axis=0)
    score_grad = attend * (
        attention_grad - jnp.sum(attend * attention_grad, axis=-1, keepdims=True)
    )

    def value_rows_grad(start, target):
        for image in range(IMG_DEV):
            for pair in range(2):
                parts = []
                for place in (2 * pair, 2 * pair + 1):
                    at = start + place
                    grads = turned[pl.ds(pl.multiple_of(at * HEAD_DIM, 8), HEAD_DIM), image : image + 1]
                    parts.append(grads * attention[pl.ds(image * 8 + at, 1), :])
                target[pair * 144 : pair * 144 + 144, image * PATCHES : (image + 1) * PATCHES] = (
                    jnp.concatenate(parts, axis=0).astype(bf16)
                )

    value_rows_grad((1 - core) * 4, away_rows)
    for image in range(IMG_DEV):
        part = score_grad[image * 8 : image * 8 + 8]
        lanes = slice(image * PATCHES, (image + 1) * PATCHES)
        away_rows[HALF_ROWS : HALF_ROWS + 16, lanes] = jnp.concatenate(
            [part, jnp.zeros((8, PATCHES), f32)], axis=0
        ).astype(bf16)
        score_rows[:, lanes] = split_low(part)

    value_send[HALF:] = jnp.zeros((LIST - HALF, 16, 128), f32)
    pair_leave, pair_arrive = new_sem(), new_sem()
    ends.append((value_send, pair_leave))
    for block in range(5):
        lanes = slice(block * 256, min(block * 256 + 256, D))
        term = dot(away_rows[...], x_all[:, lanes])
        for tile in range(block * 36, min(block * 36 + 36, HALF)):
            row, lane = tile % 18 * 16, tile // 18 * 128 - block * 256
            value_send[tile] = term[row : row + 16, lane : lane + 128]
        small_own[:, lanes] = term[HALF_ROWS : HALF_ROWS + 8]
        if block == 0:
            wait(*rows_copy)
            rows_all[0, 0] = rows_own[...]
            rows_all[0, 1] = rows_got[...]
            row_gathers = send_all(
                [(first_peer(step)[0], rows_all.at[0], rows_all.at[step]) for step in (2, 1, 3)],
                rows_all.at[1:4],
            )
        if block > 0:
            start = (block - 1) * PART
            part = slice(start, start + PART if block < 4 else LIST)
            send(other, value_send.at[part], value_got.at[part], pair_leave, pair_arrive)
    probe_part = dot(score_rows[...], keys[...])
    probe_part = jnp.where(own_head, probe_part[0:8] + probe_part[8:16], 0.0)
    probe_part = jnp.sum(probe_part, axis=0, keepdims=True) * (1.0 / math.sqrt(HEAD_DIM))
    small_own[:, D:WIDE] = jnp.zeros((8, WIDE - D), f32)
    for row in range(5):
        count = min(128, ROWS - row * 128)
        small_own[row : row + 1, D : D + count] = probe_part[:, row * 128 : row * 128 + count]
    small_copy = send_all([(other, small_own, small_got)], small_got)

    value_rows_grad(core * 4, home_rows)
    for block in range(5):
        lanes = slice(block * 256, min(block * 256 + 256, D))
        term = dot(home_rows[...], x_all[:, lanes])
        for tile in range(block * 36, min(block * 36 + 36, HALF)):
            row, lane = tile % 18 * 16, tile // 18 * 128 - block * 256
            value_own[tile] = term[row : row + 16, lane : lane + 128]
    value_own[HALF:] = jnp.zeros((LIST - HALF, 16, 128), f32)

    def piece_at(place, piece):
        return pl.ds(place * PART + piece * PIECE, PIECE)

    wait(value_got, pair_arrive)
    first_copies = []
    for ahead in (2, 1, 3, 0):
        piece = (second + ahead) % 4
        copies = []
        for step in (2, 1, 3):
            device, place = first_peer(step)
            slot = ahead * 3 + step - 1
            part = piece_at(place, piece)
            first_send[slot] = (value_own[part] + value_got[part]).astype(bf16)
            copies.append((device, first_send.at[slot], first_got.at[slot]))
        first_copies.append((ahead, send_all(copies, first_got.at[ahead * 3 : ahead * 3 + 3])))

    wait(*small_copy)
    small_pair[...] = small_own[...] + small_got[...]
    small_gathers = send_all(
        [(first_peer(step)[0], small_pair, small_all.at[step - 1]) for step in (2, 1, 3)], small_all
    )
    wait(*row_gathers)
    rows = rows_all[...].astype(f32).reshape(8, 16, D)
    embedding_grads = rows[:, :8].reshape(64, D).astype(bf16)
    pools[...] = rows[:, 8:, :ROWS].reshape(64, ROWS).T
    for block in range(3):
        at = pl.multiple_of(core * HALF_ROWS + block * 96, 32)
        term = dot(pools[pl.ds(at, 96), :].astype(bf16), embedding_grads)
        for row in range(6):
            for lane in range(9):
                out_own[lane * 18 + block * 6 + row] = term[
                    row * 16 : row * 16 + 16, lane * 128 : lane * 128 + 128
                ]
    out_own[HALF:] = jnp.zeros((LIST - HALF, 16, 128), f32)

    for piece in range(4):
        out_grid[piece] = out_own[piece_at(first, piece)].astype(bf16)
    out_copies = send_all(
        [
            (second_peer(step)[0], out_grid.at[second_peer(step)[1]], out_second.at[step - 1])
            for step in (2, 1, 3)
        ],
        out_second,
    )

    value_leave, value_arrive = new_sem(), new_sem()
    for ahead, copies in first_copies:
        wait(*copies)
        device, piece = second_peer(ahead)
        part = piece_at(first, piece)
        term = value_own[part] + value_got[part]
        for step in (1, 2, 3):
            term = term + first_got[ahead * 3 + step - 1].astype(f32)
        if ahead == 0:
            value_total[0:PIECE] = term
        else:
            value_grid[piece] = term.astype(bf16)
            send(device, value_grid.at[piece], value_second.at[ahead - 1], value_leave, value_arrive)
    ends.append((value_second, value_leave))
    wait(*small_gathers)
    small = small_pair[...] + small_all[0] + small_all[1] + small_all[2]
    small_grid[...] = jnp.zeros((4, OWNED, 16, 128), f32)
    for tile in range(SMALL_TILES):
        small_grid[tile // 2, tile % 2, 0:8] = small[:, tile * 256 : tile * 256 + 128]
        small_grid[tile // 2, tile % 2, 8:16] = small[:, tile * 256 + 128 : tile * 256 + 256]
    small_copies = send_all(
        [
            (second_peer(step)[0], small_grid.at[second_peer(step)[1]], small_second.at[step - 1])
            for step in (2, 1, 3)
        ],
        small_second,
    )

    def z_order():
        return (4, 3, 5, 2, 6, 1, 7)

    def send_third(total, got, owners):
        leave, arrive = new_sem(), new_sem()
        for step in z_order():
            device, place = third_peer(step)

            @pl.when(place < owners)
            def _():
                source = total.at[pl.ds(place * OWNED, OWNED)]
                send(device, source, got.at[step - 1], leave, arrive)

        return leave, arrive

    def send_back(total, got, leave, arrive, owners, owned, every):
        @pl.when(z < owners)
        def _():
            wait(got, arrive)
            wait(got.at[0 : owners - 1], leave)

        @pl.when(z >= owners)
        def _():
            wait(got.at[0:owners], leave)

        leave, arrive = new_sem(), new_sem()
        mine = pl.ds(z * OWNED, OWNED)

        @pl.when(z < owners)
        def _():
            result = total[mine]
            for slot in range(7):
                result = result + got[slot].astype(f32)
            total[mine] = result

        @pl.when(z < OWNERS)
        def _():
            result = total[mine].astype(bf16)
            owned[...] = result
            every[mine] = result
            for step in z_order():
                send(third_peer(step)[0], owned, every.at[mine], leave, arrive)

        return leave, arrive

    def end_back(every, leave, arrive):
        @pl.when(z < OWNERS)
        def _():
            wait(every.at[0 : (OWNERS - 1) * OWNED], arrive)
            wait(every.at[0 : 7 * OWNED], leave)

        @pl.when(z >= OWNERS)
        def _():
            wait(every.at[0 : OWNERS * OWNED], arrive)

    def send_home(part, final, leave, arrives):
        piece = final.at[core, first, part]
        for step in (2, 1, 3):
            send(first_peer(step)[0], piece, piece, leave, arrives[step - 1])

    def send_spread(every, final):
        final[core, first, second] = every[0:PIECE]
        piece = final.at[core, first, second]
        leave, arrives = new_sem(), [new_sem() for _ in range(3)]
        for step in (2, 1, 3):
            send(second_peer(step)[0], every.at[0:PIECE], piece, leave, arrives[step - 1])
        ends.append((final.at[core, first, 0:3], leave))
        home_leave, home_arrives = new_sem(), [new_sem() for _ in range(3)]
        send_home(second, final, home_leave, home_arrives)
        ends.append((final.at[core, 0:3], home_leave))
        return arrives, home_leave, home_arrives

    def forward_spread(final, arrives, home_leave, home_arrives):
        for step in (1, 3, 2):
            place = (second + 4 - step) % 4
            wait(final.at[core, first, place], arrives[step - 1])
            send_home(place, final, home_leave, home_arrives)

    def forward_homes(final, home_arrives):
        leave, arrive = new_sem(), new_sem()
        send(other, final.at[core, first], final.at[core, first], leave, arrive)
        for step in (1, 3, 2):
            part = final.at[core, (first + 4 - step) % 4]
            wait(part, home_arrives[step - 1])
            send(other, part, part, leave, arrive)
        ends.append((final.at[1 - core], leave))
        return arrive

    def unpack(final, which, target):
        for tile in range(HALF):
            place, at = tile // PART, tile % PART
            row = pl.ds(pl.multiple_of(which * HALF_ROWS + tile % 18 * 16, 16), 16)
            lane = tile // 18 * 128
            target[row, lane : lane + 128] = final[which, place, at // PIECE, at % PIECE]

    wait(*out_copies)
    out_sum = out_own[piece_at(first, second)]
    for slot in range(3):
        out_sum = out_sum + out_second[slot].astype(f32)
    out_total[0:PIECE] = out_sum
    out_total[PIECE:] = jnp.zeros((16 - PIECE, 16, 128), f32)
    out_leaving[...] = out_total[...].astype(bf16)
    out_thirds = send_third(out_leaving, out_third, OWNERS)

    wait(value_second, value_arrive)
    value_sum = value_total[0:PIECE]
    for slot in range(3):
        value_sum = value_sum + value_second[slot].astype(f32)
    value_total[0:PIECE] = value_sum
    wait(*small_copies)
    value_total[PIECE:] = jnp.zeros((16 - PIECE, 16, 128), f32)
    value_total[SMALL_AT : SMALL_AT + OWNED] = (
        small_grid[second] + small_second[0] + small_second[1] + small_second[2]
    )
    value_thirds = send_third(value_total, value_third, OWNERS + 1)

    out_back = send_back(out_total, out_third, *out_thirds, OWNERS, out_owned, out_all)

    value_back = send_back(
        value_total, value_third, *value_thirds, OWNERS + 1, value_owned, value_all
    )
    mine = small_slots.at[second]
    small_leave, small_arrive = new_sem(), new_sem()

    @pl.when(z == OWNERS)
    def _():
        small_sum = value_total[OWNERS * OWNED : (OWNERS + 1) * OWNED]
        small_owned[...] = small_sum
        small_slots[second] = small_sum
        for step in z_order():
            send(third_peer(step)[0], small_owned, mine, small_leave, small_arrive)

    end_back(out_all, *out_back)
    out_spread, *out_homes = send_spread(out_all, out_final)

    end_back(value_all, *value_back)
    value_spread, *value_homes = send_spread(value_all, value_final)
    forward_spread(out_final, out_spread, *out_homes)

    @pl.when(z == OWNERS)
    def _():
        wait(value_third, small_leave)

    @pl.when(z != OWNERS)
    def _():
        wait(mine, small_arrive)

    small_spread = send_all(
        [(second_peer(step)[0], mine, mine) for step in (2, 1, 3)], small_slots.at[0:3]
    )
    forward_spread(value_final, value_spread, *value_homes)

    wait(*visit_copies)
    caption_total = backs[0] + backs_got[0] + backs_got[1]
    caption_out[...] = (
        caption_total - own_unit * jnp.sum(own_unit * caption_total, axis=-1, keepdims=True)
    ) / own_length
    out_cross = forward_homes(out_final, out_homes[1])

    wait(*small_spread)
    small = []
    for tile in range(SMALL_TILES):
        both = small_slots[tile // 2, tile % 2]
        small += [both[0:8], both[8:16]]
    probe_sum = jnp.concatenate([small[9][row : row + 1] for row in range(5)], axis=1)
    probe_out[...] = jnp.sum(probe_sum[:, :ROWS], axis=0)
    patch_sum = jnp.concatenate(small[:9], axis=1) * (1.0 / math.sqrt(HEAD_DIM))
    probe_columns = probe.T
    for pair in range(4):
        parts = []
        for head in (2 * pair, 2 * pair + 1):
            column = probe_columns[head * HEAD_DIM : head * HEAD_DIM + HEAD_DIM, head : head + 1]
            parts.append(column * patch_sum[head : head + 1])
        key_out[pair * 144 : pair * 144 + 144, :] = jnp.concatenate(parts, axis=0).astype(bf16)
    value_cross = forward_homes(value_final, value_homes[1])

    unpack(out_final, core, out_out)
    wait(out_final.at[1 - core], out_cross)
    unpack(out_final, 1 - core, out_out)
    unpack(value_final, core, value_out)
    wait(value_final.at[1 - core], value_cross)
    unpack(value_final, 1 - core, value_out)
    for end in ends:
        wait(*end)


def finish_kernel(*refs):
    count = len(refs) // 2
    sources, targets, sem = refs[:count], refs[count : 2 * count], refs[2 * count]
    copies = [
        pltpu.make_async_copy(source, target, sem.at[slot])
        for slot, (source, target) in enumerate(zip(sources, targets))
    ]
    for copy in copies:
        copy.start()
    for copy in copies:
        copy.wait()


def in_hbm(array):
    return pltpu.with_memory_space_constraint(array, pltpu.HBM)


def on_device(
    patches, captions, probe_query, key_weight, value_weight, out_weight, logit_scale, logit_bias
):
    f32, bf16 = jnp.float32, jnp.bfloat16
    vmem = pl.BlockSpec(memory_space=pltpu.VMEM)
    smem = pl.BlockSpec(memory_space=pltpu.SMEM)
    hbm = pl.BlockSpec(memory_space=pltpu.HBM)
    dma = pltpu.SemaphoreType.DMA
    shapes = (
        jax.ShapeDtypeStruct((IMG_DEV, D), f32),
        jax.ShapeDtypeStruct((ROWS,), f32),
        jax.ShapeDtypeStruct((ROWS, D), bf16),
        jax.ShapeDtypeStruct((ROWS, D), bf16),
        jax.ShapeDtypeStruct((ROWS, D), bf16),
    )
    results = pl.pallas_call(
        whole_kernel,
        out_shape=shapes,
        in_specs=[smem, smem, hbm, hbm, hbm, hbm, hbm, hbm],
        out_specs=[vmem] * 5,
        scratch_shapes=[
            pltpu.VMEM((FLAT, D), bf16),
            pltpu.VMEM((IMG_DEV, D), bf16),
            pltpu.VMEM((ROWS,), bf16),
            pltpu.VMEM((VALUE_AT + ROWS, D), bf16),
            pltpu.VMEM((ROWS, D), bf16),
            pltpu.VMEM((FLAT, ROWS), bf16),
            pltpu.VMEM((FLAT, ROWS), bf16),
            pltpu.VMEM((64, PATCHES), f32),
            pltpu.VMEM((64, PATCHES), f32),
            pltpu.VMEM((3, 8, D), f32),
            pltpu.VMEM((3, 8, D), f32),
            pltpu.VMEM((2, 8, D), f32),
            pltpu.VMEM((ROWS, 8), f32),
            pltpu.VMEM((16, D), f32),
            pltpu.VMEM((16, D), bf16),
            pltpu.VMEM((HALF_ROWS + 16, FLAT), bf16),
            pltpu.VMEM((HALF_ROWS, FLAT), bf16),
            pltpu.VMEM((16, FLAT), bf16),
            pltpu.VMEM((8, WIDE), f32),
            pltpu.VMEM((LIST, 16, 128), f32),
            pltpu.VMEM((LIST, 16, 128), f32),
            pltpu.VMEM((LIST, 16, 128), f32),
            pltpu.VMEM((4, 2, 16, D), bf16),
            pltpu.VMEM((16, D), bf16),
            pltpu.VMEM((8, WIDE), f32),
            pltpu.VMEM((8, WIDE), f32),
            pltpu.VMEM((3, 8, WIDE), f32),
            pltpu.VMEM((ROWS, 64), f32),
            pltpu.VMEM((LIST, 16, 128), f32),
            pltpu.VMEM((12, PIECE, 16, 128), bf16),
            pltpu.VMEM((12, PIECE, 16, 128), bf16),
            pltpu.VMEM((4, PIECE, 16, 128), bf16),
            pltpu.VMEM((3, PIECE, 16, 128), bf16),
            pltpu.VMEM((4, OWNED, 16, 128), f32),
            pltpu.VMEM((3, OWNED, 16, 128), f32),
            pltpu.VMEM((16, 16, 128), f32),
            pltpu.VMEM((7, OWNED, 16, 128), f32),
            pltpu.VMEM((OWNED, 16, 128), bf16),
            pltpu.VMEM((16, 16, 128), bf16),
            pltpu.VMEM((OWNED, 16, 128), f32),
            pltpu.VMEM((4, OWNED, 16, 128), f32),
            pltpu.VMEM((2, 4, 4, PIECE, 16, 128), bf16),
            pltpu.VMEM((4, PIECE, 16, 128), bf16),
            pltpu.VMEM((3, PIECE, 16, 128), bf16),
            pltpu.VMEM((16, 16, 128), f32),
            pltpu.VMEM((16, 16, 128), bf16),
            pltpu.VMEM((7, OWNED, 16, 128), bf16),
            pltpu.VMEM((OWNED, 16, 128), bf16),
            pltpu.VMEM((16, 16, 128), bf16),
            pltpu.VMEM((2, 4, 4, PIECE, 16, 128), bf16),
            dma((9,)),
            dma((60,)),
        ],
        compiler_params=pltpu.CompilerParams(
            collective_id=0, has_side_effects=True, vmem_limit_bytes=40 * 1024 * 1024
        ),
        name="whole",
    )(
        logit_scale,
        logit_bias,
        in_hbm(patches.reshape(FLAT, D)),
        in_hbm(captions),
        in_hbm(probe_query),
        in_hbm(key_weight.T),
        in_hbm(value_weight.T),
        in_hbm(out_weight),
    )
    caption_grad, probe_grad, key_turned, value_turned, out_grad = pl.pallas_call(
        finish_kernel,
        out_shape=shapes,
        in_specs=[vmem] * 5,
        out_specs=[hbm] * 5,
        scratch_shapes=[dma((5,))],
        compiler_params=pltpu.CompilerParams(vmem_limit_bytes=8 * 1024 * 1024),
        name="finish",
    )(*results)
    return (caption_grad, probe_grad, key_turned.T, value_turned.T, out_grad)


def solution(mesh):
    placed = (P("dp", None, None), P("dp", None), P(), P(), P(), P(), P(), P())
    return jax.shard_map(
        on_device,
        mesh=mesh,
        in_specs=placed,
        out_specs=(P("dp", None), P(), P(), P(), P()),
        check_vma=False,
    )
```
